32 devices in a mesh: groups: 2 (over y), row: 8 (over z, x), col: 2 (over core).
Axes of the slice: x: 2, y: 2, z: 4, core: 2. Of those that a mesh axis runs over, the one named last changes fastest.
Arguments:
- effects: float32 [16384, 512], P(('groups', 'row', 'col')), parts along dimension 0, may hold values from -6 to 6
- zscores: float32 [16384, 512], P(('groups', 'row', 'col')), parts along dimension 0, may hold values from -6 to 6
- ridge: float32 [1024], P('groups'), parts along dimension 0, may hold values from 0.1 to 1
- band_tiles: bfloat16 [128, 9, 128, 128], P(('groups', 'row', 'col')), parts along dimension 0, may hold values from -0.1875 to 0.1875
- lr_tiles: bfloat16 [256, 128, 128], P(('groups', 'row', 'col')), parts along dimension 0, may hold values from -0.0625 to 0.0625
- lr_local: int32 [256], P(('groups', 'row', 'col')), parts along dimension 0, may hold values from 0 to 3
- lr_hub: int32 [256], P(('groups', 'row', 'col')), parts along dimension 0, may hold values from 0 to 3
- hub_blocks: int32 [8], P('groups'), parts along dimension 0, may hold values from 0 to 63, as said below
Outputs:
- fitted: float32 [16384, 512], P(('groups', 'row', 'col')), parts along dimension 0
The draws below stay inside these ranges and needn't reach their ends.
There are 2 independent parts, one for each index of `groups`. The reference program is written for one: setup_inputs(seed, part) draws one part's arguments, and reference() takes and returns one part's arrays. A program takes and returns all parts, laid end to end along the dimension named above; each array names one. Nothing has to cross between parts.
Inputs may be any that keep to these rules, and one draw needn't show every extreme that they name: `hub_blocks`: the 4 entries are distinct block numbers.
All inputs are finite; a program needn't handle non-finite values.
Results may differ from the reference program's by a relative error of at most 0.0017.
Values may be sent and summed in bfloat16 or wider, within the bound.
No kernel may reach another device: no remote copies, remote signals or barrier semaphores. Data moves between devices by JAX's collectives and lax.ppermute only.
A program may use at most 64 MiB of HBM per device.

```python
import math
import jax
import jax.numpy as jnp
from jax import lax

TR = 512
TILE = 128
BLK_DEV = 4
W = 4
LR_DEV = 8
HUBS = 4
ITERS = 2
NBLK = 64
VARIANTS = 8192
LR_ALL = 128


def draw_hub_blocks(key, part):
    order = jax.random.permutation(jax.random.fold_in(key, 17), NBLK)
    return order[:HUBS].astype(jnp.int32)


def touch_ends(array, stream_key, least, top_value):
    longest = array.shape.index(max(array.shape))
    spots = []
    for shift in (0, 1):
        where = [jax.random.randint(jax.random.fold_in(stream_key, axis), (), 0, length) for axis, length in enumerate(array.shape)]
        where[longest] = (where[longest] + shift) % array.shape[longest]
        spots.append(tuple(where))
    return array.at[spots[0]].set(least).at[spots[1]].set(top_value)


def levels(own_key, dims, pieces, smallest, high):
    def one(axis_at, blocks):
        steps = jax.random.uniform(jax.random.fold_in(jax.random.fold_in(own_key, 6), axis_at), (blocks,), jnp.float32, smallest / len(pieces), high / len(pieces))
        return jnp.repeat(jnp.exp(steps), dims[axis_at] // blocks).reshape((-1,) + (1,) * (len(dims) - axis_at - 1))

    level = one(*pieces[0])
    for cut in pieces[1:]:
        level = level * one(*cut)
    return level


def normal_values(rng, shape, width, most, split=(), held_as=jnp.bfloat16):
    loudness = levels(rng, shape, split, -0.22, 0.18) if split else 1.0
    drawn = jax.random.normal(rng, shape, jnp.float32) * width * loudness
    return jnp.minimum(jnp.maximum(drawn, -most), most).astype(held_as)


def setup_inputs(seed: int = 0, part: int = 0) -> dict:
    arg_keys = jax.random.split(jax.random.key(seed), 9)
    own_keys = jax.random.split(jax.random.fold_in(arg_keys[8], part), 9)
    effects = normal_values(own_keys[0], (VARIANTS, TR), 1.0, 6.0, ((0, 16),), jnp.float32)
    zscores = normal_values(own_keys[1], (VARIANTS, TR), 1.0, 6.0, ((0, 16),), jnp.float32)
    ridge = jnp.clip(jnp.exp(jax.random.uniform(own_keys[2], (TR,), jnp.float32, math.log(0.1), math.log(1.0))), 0.1, 1.0)
    band_tiles = normal_values(own_keys[3], (NBLK, 2 * W + 1, TILE, TILE), (TILE * (2 * W + 1)) ** -0.5, 0.1875, ((0, 16),))
    lr_tiles = normal_values(own_keys[4], (LR_ALL, TILE, TILE), (TILE * 64) ** -0.5, 0.0625, ((0, 16),))
    lr_local = touch_ends(jax.random.randint(own_keys[5], (LR_ALL,), 0, BLK_DEV), jax.random.fold_in(own_keys[5], 1), 0, BLK_DEV - 1).astype(jnp.int32)
    lr_hub = touch_ends(jax.random.randint(own_keys[6], (LR_ALL,), 0, HUBS), jax.random.fold_in(own_keys[6], 1), 0, HUBS - 1).astype(jnp.int32)
    hub_blocks = draw_hub_blocks(jax.random.fold_in(jax.random.fold_in(arg_keys[8], part), 71), part)
    return {"effects": effects, "zscores": zscores, "ridge": ridge, "band_tiles": band_tiles, "lr_tiles": lr_tiles, "lr_local": lr_local, "lr_hub": lr_hub, "hub_blocks": hub_blocks}


step_size = 0.5


def reference(effects, zscores, ridge, band_tiles, lr_tiles, lr_local, lr_hub, hub_blocks):
    slot_ids = jnp.arange(LR_ALL, dtype=jnp.int32)
    row_block = ((slot_ids // LR_DEV) * BLK_DEV + lr_local).astype(jnp.int32)
    hub_block = hub_blocks[lr_hub].astype(jnp.int32)
    band_float = band_tiles.astype(jnp.float32)
    far_float = lr_tiles.astype(jnp.float32)
    current = effects
    for sweep in range(ITERS):
        rounded = lax.optimization_barrier(current.astype(jnp.bfloat16))
        panels = rounded.astype(jnp.float32).reshape(NBLK, TILE, TR)
        padded = jnp.pad(panels, ((W, W), (0, 0), (0, 0)))
        gradient = jnp.zeros((NBLK, TILE, TR), jnp.float32)
        for offset in range(2 * W + 1):
            gradient = gradient + jnp.einsum("bij,bjt->bit", band_float[:, offset], padded[offset:offset + NBLK], precision=lax.Precision.HIGHEST)
        far_terms = jnp.einsum("sij,sjt->sit", far_float, panels[hub_block], precision=lax.Precision.HIGHEST)
        gradient = gradient.at[row_block].add(far_terms)
        back_terms = jnp.einsum("sji,sjt->sit", far_float, panels[row_block], precision=lax.Precision.HIGHEST)
        gradient = gradient.at[hub_block].add(back_terms)
        gradient = gradient.reshape(VARIANTS, TR) + ridge[None, :] * current - zscores
        current = current - step_size * gradient
    return current
```

```python
import functools

import jax
import jax.numpy as jnp
from jax import lax
from jax.experimental import pallas as pl
from jax.experimental.pallas import tpu as pltpu
from jax.sharding import PartitionSpec as P

ITERS = 2
STEP = 0.5
F32 = jnp.float32
BF16 = jnp.bfloat16
VMEM = pl.BlockSpec(memory_space=pltpu.VMEM)
SMEM = pl.BlockSpec(memory_space=pltpu.SMEM)


def dot(a, b):
    return jnp.dot(a, b, preferred_element_type=F32)


def dot_t(a, b):
    return lax.dot_general(a, b, (((0,), (0,)), ((), ())), preferred_element_type=F32)


class Place:
    def __init__(self, block, blocks, cores):
        self.chip = block // (blocks * cores)
        self.core = (block // blocks) % cores
        self.blk = block % blocks


def back_terms(local_ref, hub_ref, lr_ref, panel_ref, acc_ref, out_ref):
    tile = lr_ref.shape[1]
    acc_ref[...] = jnp.zeros_like(acc_ref)
    for s in range(lr_ref.shape[0]):
        rows = pl.ds(pl.multiple_of(local_ref[s] * tile, tile), tile)
        hub = pl.ds(pl.multiple_of(hub_ref[s] * tile, tile), tile)
        acc_ref[hub, :] += dot_t(lr_ref[s], panel_ref[rows, :])
    out_ref[...] = acc_ref[...].astype(BF16)


def first_kernel(local_ref, hub_ref, effects_ref, lr_ref, panel_ref, back_ref, acc_ref):
    panel_ref[...] = effects_ref[...].astype(BF16)
    back_terms(local_ref, hub_ref, lr_ref, panel_ref, acc_ref, back_ref)


def pick_kernel(cores, tile, blocks_ref, mine_ref, other_ref, back_ref, back_other_ref, out_ref):
    me, core = lax.axis_index("row"), lax.axis_index("col")
    blocks = mine_ref.shape[0] // tile
    count = out_ref.shape[0] // tile
    for j in range(count):
        hub = core * count + j
        place = Place(blocks_ref[hub], blocks, cores)
        out = pl.ds(j * tile, tile)
        src = pl.ds(pl.multiple_of(place.blk * tile, tile), tile)
        row = pl.ds(pl.multiple_of(hub * tile, tile), tile)
        here = place.chip == me

        @pl.when(here & (place.core == core))
        def _():
            out_ref[out, :] = mine_ref[src, :]

        @pl.when(here & (place.core != core))
        def _():
            out_ref[out, :] = other_ref[src, :]

        @pl.when(jnp.logical_not(here))
        def _():
            both = back_ref[row, :].astype(F32) + back_other_ref[row, :].astype(F32)
            out_ref[out, :] = both.astype(BF16)


def merge_kernel(cores, tile, per_chip, blocks_ref, in_ref, out_ref):
    me, core = lax.axis_index("row"), lax.axis_index("col")
    chips, rows, _ = in_ref.shape
    hub = (core * (chips * rows) + me * rows) // tile
    owner = blocks_ref[hub] // per_chip

    def add(p, total):
        return total + jnp.where(p == owner, 0.0, in_ref[p].astype(F32))

    def put(p, carry):
        out_ref[p] = jnp.where(p == owner, total, state)
        return carry

    zero = jnp.zeros(in_ref.shape[1:], F32)
    total = lax.fori_loop(0, chips, add, zero, unroll=chips <= 16).astype(BF16)
    state = in_ref[owner]
    lax.fori_loop(0, chips, put, 0, unroll=chips <= 16)


def step_kernel(
    cores,
    last,
    blocks_ref,
    local_ref,
    hub_ref,
    current_ref,
    zscores_ref,
    ridge_ref,
    band_ref,
    lr_ref,
    mine_ref,
    other_ref,
    outer_ref,
    half_ref,
    half_other_ref,
    back_ref,
    back_other_ref,
    *rest,
):
    if last:
        next_ref, window_ref, state_ref, grad_ref = rest
    else:
        next_ref, panel_ref, back_out_ref, window_ref, state_ref, grad_ref, acc_ref = rest
    me, core = lax.axis_index("row"), lax.axis_index("col")
    blocks, width, tile, _ = band_ref.shape
    rows = blocks * tile
    hubs = blocks_ref.shape[0]
    per_half = hubs // cores
    reach = (width - 1) // 2 * tile

    window_ref[reach : reach + rows, :] = mine_ref[...]

    @pl.when(core == 0)
    def _():
        window_ref[:reach, :] = outer_ref[rows - reach :, :]
        window_ref[reach + rows :, :] = other_ref[:reach, :]

    @pl.when(core != 0)
    def _():
        window_ref[:reach, :] = other_ref[rows - reach :, :]
        window_ref[reach + rows :, :] = outer_ref[:reach, :]

    for b in range(blocks):
        tiles = jnp.concatenate([band_ref[b, o] for o in range(width)], axis=1)
        grad_ref[b * tile : (b + 1) * tile, :] = dot(
            tiles, window_ref[b * tile : (b + width) * tile, :]
        )

    for hub in range(hubs):
        place = Place(blocks_ref[hub], blocks, cores)
        here = place.chip == me
        near = core == hub // per_half
        src = pl.ds(hub % per_half * tile, tile)
        dst = pl.ds(hub * tile, tile)
        own = pl.ds(pl.multiple_of(place.blk * tile, tile), tile)

        @pl.when(jnp.logical_not(here))
        def _():
            state_ref[dst, :] = jnp.where(near, half_ref[src, :], half_other_ref[src, :])

        @pl.when(here & (place.core != core))
        def _():
            state_ref[dst, :] = other_ref[own, :]

        @pl.when(here & (place.core == core))
        def _():
            state_ref[dst, :] = mine_ref[own, :]
            far = jnp.where(near, half_ref[src, :], half_other_ref[src, :])
            grad_ref[own, :] += (
                far.astype(F32) + back_ref[dst, :].astype(F32) + back_other_ref[dst, :].astype(F32)
            )

    for s in range(lr_ref.shape[0]):
        row = pl.ds(pl.multiple_of(local_ref[s] * tile, tile), tile)
        col = pl.ds(pl.multiple_of(hub_ref[s] * tile, tile), tile)
        grad_ref[row, :] += dot(lr_ref[s], state_ref[col, :])

    current = current_ref[...]
    gradient = grad_ref[...] + (ridge_ref[...] * current - zscores_ref[...])
    following = current - STEP * gradient
    next_ref[...] = following
    if not last:
        panel_ref[...] = following.astype(BF16)
        back_terms(local_ref, hub_ref, lr_ref, panel_ref, acc_ref, back_out_ref)


def shards(rows_dev, cores, effects, zscores, ridge, band, lr, lr_local, lr_hub, hub_blocks):
    blocks, _, tile, _ = band.shape
    rows, traits = effects.shape
    hubs = hub_blocks.shape[0]
    hub_rows = hubs * tile
    half = hub_rows // cores
    total = rows_dev * cores
    params = pltpu.CompilerParams(vmem_limit_bytes=48 * 1024 * 1024)
    panel_type = jax.ShapeDtypeStruct((rows, traits), BF16)
    back_type = jax.ShapeDtypeStruct((hub_rows, traits), BF16)
    ridge = ridge[None, :]

    odd = [(i, i + 1) for i in range(cores - 1, total - 1, cores)]
    odd = odd + [(j, i) for i, j in odd]
    swap = [(0, 1), (1, 0)]

    def other_core(x):
        return lax.ppermute(x, "col", swap)

    def exchange(x):
        x = x.reshape(rows_dev, half // rows_dev, traits)
        return lax.all_to_all(x, "row", 0, 0)

    panels, back = pl.pallas_call(
        first_kernel,
        out_shape=(panel_type, back_type),
        in_specs=[SMEM, SMEM, VMEM, VMEM],
        out_specs=(VMEM, VMEM),
        scratch_shapes=[pltpu.VMEM((hub_rows, traits), F32)],
        compiler_params=params,
        name="first",
    )(lr_local, lr_hub, effects, lr)

    current = effects
    for sweep in range(ITERS):
        last = sweep == ITERS - 1
        other = other_core(panels)
        back_other = other_core(back)
        outer = lax.ppermute(panels, ("row", "col"), odd)
        chosen = pl.pallas_call(
            functools.partial(pick_kernel, cores, tile),
            out_shape=jax.ShapeDtypeStruct((half, traits), BF16),
            in_specs=[SMEM, VMEM, VMEM, VMEM, VMEM],
            out_specs=VMEM,
            compiler_params=params,
            name="pick",
        )(hub_blocks, panels, other, back, back_other)
        gathered = exchange(chosen)
        merged = pl.pallas_call(
            functools.partial(merge_kernel, cores, tile, blocks * cores),
            out_shape=jax.ShapeDtypeStruct(gathered.shape, BF16),
            in_specs=[SMEM, VMEM],
            out_specs=VMEM,
            compiler_params=params,
            name="merge",
        )(hub_blocks, gathered)
        mine = exchange(merged).reshape(half, traits)
        theirs = other_core(mine)
        out_shape = [jax.ShapeDtypeStruct((rows, traits), F32)]
        scratch = [
            pltpu.VMEM((rows + 2 * ((band.shape[1] - 1) // 2) * tile, traits), BF16),
            pltpu.VMEM((hub_rows, traits), BF16),
            pltpu.VMEM((rows, traits), F32),
        ]
        if not last:
            out_shape += [panel_type, back_type]
            scratch += [pltpu.VMEM((hub_rows, traits), F32)]
        result = pl.pallas_call(
            functools.partial(step_kernel, cores, last),
            out_shape=tuple(out_shape),
            in_specs=[SMEM] * 3 + [VMEM] * 12,
            out_specs=(VMEM,) * len(out_shape),
            scratch_shapes=scratch,
            compiler_params=params,
            name="step",
        )(
            hub_blocks,
            lr_local,
            lr_hub,
            current,
            zscores,
            ridge,
            band,
            lr,
            panels,
            other,
            outer,
            mine,
            theirs,
            back,
            back_other,
        )
        if last:
            return result[0]
        current, panels, back = result


def solution(mesh):
    every = ("groups", "row", "col")
    placed = (
        P(every, None),
        P(every, None),
        P("groups"),
        P(every, None, None, None),
        P(every, None, None),
        P(every),
        P(every),
        P("groups"),
    )
    return jax.shard_map(
        functools.partial(shards, mesh.shape["row"], mesh.shape["col"]),
        mesh=mesh,
        in_specs=placed,
        out_specs=P(every, None),
        check_vma=False,
    )
```

```python
import functools

import jax
import jax.numpy as jnp
from jax import lax
from jax.experimental import pallas as pl
from jax.experimental.pallas import tpu as pltpu
from jax.sharding import PartitionSpec as P

ITERS = 2
STEP = 0.5
F32 = jnp.float32
BF16 = jnp.bfloat16
WIDE = pltpu.CompilerParams(vmem_limit_bytes=58 * 2**20)
NARROW = pltpu.CompilerParams(vmem_limit_bytes=12 * 2**20)
VMEM = pl.BlockSpec(memory_space=pltpu.VMEM)
HBM = pl.BlockSpec(memory_space=pltpu.HBM)
ANY = pl.BlockSpec(memory_space=pl.ANY)
SMEM = pl.BlockSpec(memory_space=pltpu.SMEM)


def dot(a, b):
    return jnp.dot(a, b, preferred_element_type=F32)


def dot_t(a, b):
    return lax.dot_general(a, b, (((0,), (0,)), ((), ())), preferred_element_type=F32)


class Place:
    def __init__(self, block, blocks, cores):
        self.chip = block // (blocks * cores)
        self.core = (block // blocks) % cores
        self.blk = block % blocks


def back_terms(local_ref, hub_ref, lr_ref, panel_ref, acc_ref, out_ref):
    tile = lr_ref.shape[1]
    acc_ref[...] = jnp.zeros_like(acc_ref)
    for s in range(lr_ref.shape[0]):
        rows = pl.ds(pl.multiple_of(local_ref[s] * tile, tile), tile)
        hub = pl.ds(pl.multiple_of(hub_ref[s] * tile, tile), tile)
        acc_ref[hub, :] += dot_t(lr_ref[s], panel_ref[rows, :])
    out_ref[...] = acc_ref[...].astype(BF16)


def fetch(pairs, sems):
    copies = [pltpu.make_async_copy(a, b, sems.at[n]) for n, (a, b) in enumerate(pairs)]
    for copy in copies:
        copy.start()
    return copies


def first_kernel(*refs):
    sources, (panel_ref, back_ref, acc_ref), held, sems = refs[:4], refs[4:7], refs[7:11], refs[11]
    for copy in fetch(list(zip(sources, held)), sems):
        copy.wait()
    local_ref, hub_ref, effects_ref, lr_ref = held
    panel_ref[...] = effects_ref[...].astype(BF16)
    back_terms(local_ref, hub_ref, lr_ref, panel_ref, acc_ref, back_ref)


def pick_kernel(cores, tile, blocks_ref, mine_ref, other_ref, back_ref, back_other_ref, out_ref):
    me, core = lax.axis_index("row"), lax.axis_index("col")
    blocks = mine_ref.shape[0] // tile
    count = out_ref.shape[0] // tile
    for j in range(count):
        hub = core * count + j
        place = Place(blocks_ref[hub], blocks, cores)
        out = pl.ds(j * tile, tile)
        src = pl.ds(pl.multiple_of(place.blk * tile, tile), tile)
        row = pl.ds(pl.multiple_of(hub * tile, tile), tile)
        here = place.chip == me

        @pl.when(here & (place.core == core))
        def _():
            out_ref[out, :] = mine_ref[src, :]

        @pl.when(here & (place.core != core))
        def _():
            out_ref[out, :] = other_ref[src, :]

        @pl.when(jnp.logical_not(here))
        def _():
            both = back_ref[row, :].astype(F32) + back_other_ref[row, :].astype(F32)
            out_ref[out, :] = both.astype(BF16)


def merge_kernel(cores, tile, per_chip, blocks_ref, in_ref, outer_ref, out_ref):
    del outer_ref
    me, core = lax.axis_index("row"), lax.axis_index("col")
    chips, rows, _ = in_ref.shape
    hub = (core * (chips * rows) + me * rows) // tile
    owner = blocks_ref[hub] // per_chip

    def add(p, total):
        return total + jnp.where(p == owner, 0.0, in_ref[p].astype(F32))

    def put(p, carry):
        out_ref[p] = jnp.where(p == owner, total, state)
        return carry

    zero = jnp.zeros(in_ref.shape[1:], F32)
    total = lax.fori_loop(0, chips, add, zero, unroll=chips <= 16).astype(BF16)
    state = in_ref[owner]
    lax.fori_loop(0, chips, put, 0, unroll=chips <= 16)


def band_kernel(
    cores,
    blocks_ref,
    current_hbm,
    zscores_hbm,
    ridge_hbm,
    band_hbm,
    mine_hbm,
    other_hbm,
    outer_hbm,
    back_hbm,
    back_other_hbm,
    next_ref,
    state_ref,
    window_ref,
    current_ref,
    zscores_ref,
    ridge_ref,
    band_ref,
    back_ref,
    back_other_ref,
    sems,
):
    me, core = lax.axis_index("row"), lax.axis_index("col")
    blocks, width, tile, _ = band_ref.shape
    rows = blocks * tile
    reach = (width - 1) // 2 * tile
    first, middle, last = pl.ds(0, reach), pl.ds(reach, rows), pl.ds(reach + rows, reach)
    head, tail = pl.ds(0, reach), pl.ds(rows - reach, reach)

    copies = fetch(
        [
            (mine_hbm, window_ref.at[middle]),
            (band_hbm, band_ref),
            (current_hbm, current_ref),
            (zscores_hbm, zscores_ref),
            (ridge_hbm, ridge_ref),
            (back_hbm, back_ref),
            (back_other_hbm, back_other_ref),
        ],
        sems,
    )
    before, after = sems.at[len(copies)], sems.at[len(copies) + 1]

    @pl.when(core == 0)
    def _():
        pltpu.make_async_copy(outer_hbm.at[tail], window_ref.at[first], before).start()
        pltpu.make_async_copy(other_hbm.at[head], window_ref.at[last], after).start()

    @pl.when(core != 0)
    def _():
        pltpu.make_async_copy(other_hbm.at[tail], window_ref.at[first], before).start()
        pltpu.make_async_copy(outer_hbm.at[head], window_ref.at[last], after).start()

    for copy in copies:
        copy.wait()
    pltpu.make_async_copy(other_hbm.at[tail], window_ref.at[first], before).wait()
    pltpu.make_async_copy(other_hbm.at[head], window_ref.at[last], after).wait()

    for b in range(blocks):
        out = slice(b * tile, (b + 1) * tile)
        tiles = jnp.concatenate([band_ref[b, o] for o in range(width)], axis=1)
        gradient = dot(tiles, window_ref[b * tile : (b + width) * tile, :])
        current = current_ref[out, :]
        gradient += ridge_ref[...] * current - zscores_ref[out, :]
        next_ref[out, :] = current - STEP * gradient

    for hub in range(blocks_ref.shape[0]):
        place = Place(blocks_ref[hub], blocks, cores)
        here = place.chip == me
        row = pl.ds(hub * tile, tile)
        own = pl.ds(pl.multiple_of(place.blk * tile, tile), tile)
        middle = pl.ds(pl.multiple_of(reach + place.blk * tile, tile), tile)
        shift = jnp.where(core == 0, rows, -rows)
        beside = pl.ds(pl.multiple_of(reach + place.blk * tile + shift, tile), tile)

        @pl.when(here & (place.core == core))
        def _():
            state_ref[row, :] = window_ref[middle, :]
            both = back_ref[row, :].astype(F32) + back_other_ref[row, :].astype(F32)
            next_ref[own, :] -= STEP * both

        @pl.when(here & (place.core != core))
        def _():
            state_ref[row, :] = window_ref[beside, :]

        @pl.when(jnp.logical_not(here))
        def _():
            state_ref[row, :] = jnp.zeros_like(state_ref[row, :])


def step_kernel(
    cores,
    last,
    blocks_ref,
    local_ref,
    hub_ref,
    partial_ref,
    lr_ref,
    own_state_ref,
    half_ref,
    half_other_ref,
    *rest,
):
    if last:
        next_ref, state_ref, grad_ref = rest
    else:
        next_ref, panel_ref, back_out_ref, state_ref, grad_ref, acc_ref = rest
    me, core = lax.axis_index("row"), lax.axis_index("col")
    tile = lr_ref.shape[1]
    blocks = next_ref.shape[0] // tile
    hubs = blocks_ref.shape[0]
    per_half = hubs // cores
    grad_ref[...] = jnp.zeros_like(grad_ref)

    for hub in range(hubs):
        place = Place(blocks_ref[hub], blocks, cores)
        here = place.chip == me
        near = core == hub // per_half
        src = pl.ds(hub % per_half * tile, tile)
        dst = pl.ds(hub * tile, tile)
        own = pl.ds(pl.multiple_of(place.blk * tile, tile), tile)
        came = jnp.where(near, half_ref[src, :], half_other_ref[src, :])

        @pl.when(here)
        def _():
            state_ref[dst, :] = own_state_ref[dst, :]

        @pl.when(here & (place.core == core))
        def _():
            grad_ref[own, :] = came.astype(F32)

        @pl.when(jnp.logical_not(here))
        def _():
            state_ref[dst, :] = came

    for s in range(lr_ref.shape[0]):
        row = pl.ds(pl.multiple_of(local_ref[s] * tile, tile), tile)
        col = pl.ds(pl.multiple_of(hub_ref[s] * tile, tile), tile)
        grad_ref[row, :] += dot(lr_ref[s], state_ref[col, :])

    following = partial_ref[...] - STEP * grad_ref[...]
    next_ref[...] = following
    if not last:
        panel_ref[...] = following.astype(BF16)
        back_terms(local_ref, hub_ref, lr_ref, panel_ref, acc_ref, back_out_ref)


def shards(rows_dev, cores, effects, zscores, ridge, band, lr, lr_local, lr_hub, hub_blocks):
    blocks, _, tile, _ = band.shape
    rows, traits = effects.shape
    hubs = hub_blocks.shape[0]
    hub_rows = hubs * tile
    half = hub_rows // cores
    total = rows_dev * cores
    panel_type = jax.ShapeDtypeStruct((rows, traits), BF16)
    back_type = jax.ShapeDtypeStruct((hub_rows, traits), BF16)
    ridge = ridge[None, :]

    odd = [(i, i + 1) for i in range(cores - 1, total - 1, cores)]
    odd = odd + [(j, i) for i, j in odd]
    swap = [(0, 1), (1, 0)]

    def other_core(x):
        return lax.ppermute(x, "col", swap)

    def exchange(x):
        x = x.reshape(rows_dev, half // rows_dev, traits)
        return lax.all_to_all(x, "row", 0, 0)

    panels, back = pl.pallas_call(
        first_kernel,
        out_shape=(panel_type, back_type),
        in_specs=[HBM] * 4,
        out_specs=(VMEM, VMEM),
        scratch_shapes=[
            pltpu.VMEM((hub_rows, traits), F32),
            pltpu.SMEM(lr_local.shape, jnp.int32),
            pltpu.SMEM(lr_hub.shape, jnp.int32),
            pltpu.VMEM(effects.shape, F32),
            pltpu.VMEM(lr.shape, BF16),
            pltpu.SemaphoreType.DMA((4,)),
        ],
        compiler_params=WIDE,
        name="first",
    )(lr_local, lr_hub, effects, lr)

    current = effects
    for sweep in range(ITERS):
        last = sweep == ITERS - 1
        other = other_core(panels)
        back_other = other_core(back)
        outer = lax.ppermute(panels, ("row", "col"), odd)
        chosen = pl.pallas_call(
            functools.partial(pick_kernel, cores, tile),
            out_shape=jax.ShapeDtypeStruct((half, traits), BF16),
            in_specs=[SMEM, VMEM, VMEM, VMEM, VMEM],
            out_specs=VMEM,
            compiler_params=NARROW,
            name="pick",
        )(hub_blocks, panels, other, back, back_other)
        gathered = exchange(chosen)
        merged = pl.pallas_call(
            functools.partial(merge_kernel, cores, tile, blocks * cores),
            out_shape=jax.ShapeDtypeStruct(gathered.shape, BF16),
            in_specs=[SMEM, VMEM, ANY],
            out_specs=VMEM,
            compiler_params=NARROW,
            name="merge",
        )(hub_blocks, gathered, outer)
        partial, own_state = pl.pallas_call(
            functools.partial(band_kernel, cores),
            out_shape=(jax.ShapeDtypeStruct((rows, traits), F32), back_type),
            in_specs=[SMEM] + [HBM] * 9,
            out_specs=(VMEM, VMEM),
            scratch_shapes=[
                pltpu.VMEM((rows + (band.shape[1] - 1) * tile, traits), BF16),
                pltpu.VMEM(current.shape, F32),
                pltpu.VMEM(zscores.shape, F32),
                pltpu.VMEM(ridge.shape, F32),
                pltpu.VMEM(band.shape, BF16),
                pltpu.VMEM(back.shape, BF16),
                pltpu.VMEM(back.shape, BF16),
                pltpu.SemaphoreType.DMA((9,)),
            ],
            compiler_params=WIDE,
            cost_estimate=pl.CostEstimate(
                flops=2 * band.size * traits, bytes_accessed=8 * 2**20, transcendentals=0
            ),
            name="band",
        )(hub_blocks, current, zscores, ridge, band, panels, other, outer, back, back_other)
        mine = exchange(merged).reshape(half, traits)
        mine, partial, own_state = lax.optimization_barrier((mine, partial, own_state))
        theirs = other_core(mine)
        out_shape = [jax.ShapeDtypeStruct((rows, traits), F32)]
        scratch = [
            pltpu.VMEM((hub_rows, traits), BF16),
            pltpu.VMEM((rows, traits), F32),
        ]
        if not last:
            out_shape += [panel_type, back_type]
            scratch += [pltpu.VMEM((hub_rows, traits), F32)]
        result = pl.pallas_call(
            functools.partial(step_kernel, cores, last),
            out_shape=tuple(out_shape),
            in_specs=[SMEM] * 3 + [VMEM] * 5,
            out_specs=(VMEM,) * len(out_shape),
            scratch_shapes=scratch,
            compiler_params=NARROW,
            name="step",
        )(
            hub_blocks,
            lr_local,
            lr_hub,
            partial,
            lr,
            own_state,
            mine,
            theirs,
        )
        if last:
            return result[0]
        current, panels, back = result


def solution(mesh):
    every = ("groups", "row", "col")
    placed = (
        P(every, None),
        P(every, None),
        P("groups"),
        P(every, None, None, None),
        P(every, None, None),
        P(every),
        P(every),
        P("groups"),
    )
    return jax.shard_map(
        functools.partial(shards, mesh.shape["row"], mesh.shape["col"]),
        mesh=mesh,
        in_specs=placed,
        out_specs=P(every, None),
        check_vma=False,
    )
```

```python
import functools

import jax
import jax.numpy as jnp
from jax import lax
from jax.experimental import pallas as pl
from jax.experimental.pallas import tpu as pltpu
from jax.sharding import PartitionSpec as P

ITERS = 2
STEP = 0.5
F32 = jnp.float32
BF16 = jnp.bfloat16
FIRST = pltpu.CompilerParams(vmem_limit_bytes=58 * 2**20)
MERGE = pltpu.CompilerParams(vmem_limit_bytes=12 * 2**20)
BAND = pltpu.CompilerParams(vmem_limit_bytes=58 * 2**20)
UPDATE = pltpu.CompilerParams(vmem_limit_bytes=53850 * 2**10)
VMEM = pl.BlockSpec(memory_space=pltpu.VMEM)
HBM = pl.BlockSpec(memory_space=pltpu.HBM)
ANY = pl.BlockSpec(memory_space=pl.ANY)
SMEM = pl.BlockSpec(memory_space=pltpu.SMEM)


def dot(a, b):
    return jnp.dot(a, b, preferred_element_type=F32)


def dot_t(a, b):
    return lax.dot_general(a, b, (((0,), (0,)), ((), ())), preferred_element_type=F32)


class Place:
    def __init__(self, block, blocks, cores):
        self.chip = block // (blocks * cores)
        self.core = (block // blocks) % cores
        self.blk = block % blocks


def back_terms(local_ref, hub_ref, lr_ref, panel_ref, term_ref, acc_ref, out_ref):
    count, tile, _ = lr_ref.shape
    for s in range(count):
        rows = pl.ds(pl.multiple_of(local_ref[s] * tile, tile), tile)
        term_ref[s] = dot_t(lr_ref[s], panel_ref[rows, :])
    acc_ref[...] = jnp.zeros_like(acc_ref)
    for s in range(count):
        acc_ref[pl.ds(pl.multiple_of(hub_ref[s] * tile, tile), tile), :] += term_ref[s]
    out_ref[...] = acc_ref[...].astype(BF16)


def fetch(pairs, sems):
    copies = [pltpu.make_async_copy(a, b, sems.at[n]) for n, (a, b) in enumerate(pairs)]
    for copy in copies:
        copy.start()
    return copies


def contributions(cores, blocks_ref, back_ref, panel_ref, keep_ref, send_ref):
    me, core = lax.axis_index("row"), lax.axis_index("col")
    hubs = blocks_ref.shape[0]
    tile = back_ref.shape[0] // hubs
    blocks = panel_ref.shape[0] // tile
    per_half = hubs // cores

    def write(ref, half):
        for j in range(per_half):
            hub = half * per_half + j
            place = Place(blocks_ref[hub], blocks, cores)
            out = pl.ds(j * tile, tile)
            row = pl.ds(pl.multiple_of(hub * tile, tile), tile)
            own = pl.ds(pl.multiple_of(place.blk * tile, tile), tile)
            here, near = place.chip == me, place.core == core

            @pl.when(jnp.logical_not(here))
            def _():
                ref[out, :] = back_ref[row, :]

            @pl.when(here & near)
            def _():
                ref[out, :] = panel_ref[own, :]

            @pl.when(here & jnp.logical_not(near))
            def _():
                ref[out, :] = jnp.zeros_like(ref[out, :])

    write(keep_ref, core)
    write(send_ref, 1 - core)


def first_kernel(cores, *refs):
    sources, (panel_ref, back_ref, keep_ref, send_ref, acc_ref) = refs[:5], refs[5:10]
    held, (sems, term_ref) = refs[10:15], refs[15:]
    for copy in fetch(list(zip(sources, held)), sems):
        copy.wait()
    blocks_ref, local_ref, hub_ref, effects_ref, lr_ref = held
    panel_ref[...] = effects_ref[...].astype(BF16)
    back_terms(local_ref, hub_ref, lr_ref, panel_ref, term_ref, acc_ref, back_ref)
    contributions(cores, blocks_ref, back_ref, panel_ref, keep_ref, send_ref)


def merge_kernel(cores, tile, per_chip, blocks_ref, in_ref, *rest):
    *_, out_ref = rest
    me, core = lax.axis_index("row"), lax.axis_index("col")
    chips, rows, _ = in_ref.shape
    hub = (core * (chips * rows) + me * rows) // tile
    owner = blocks_ref[hub] // per_chip

    def add(p, total):
        return total + jnp.where(p == owner, 0.0, in_ref[p].astype(F32))

    def put(p, carry):
        out_ref[p] = jnp.where(p == owner, total, state)
        return carry

    zero = jnp.zeros(in_ref.shape[1:], F32)
    total = lax.fori_loop(0, chips, add, zero, unroll=chips <= 16).astype(BF16)
    state = in_ref[owner]
    lax.fori_loop(0, chips, put, 0, unroll=chips <= 16)


def band_kernel(
    cores,
    blocks_ref,
    local_ref,
    hub_ref,
    current_hbm,
    zscores_hbm,
    ridge_hbm,
    band_hbm,
    mine_hbm,
    other_hbm,
    back_hbm,
    back_other_hbm,
    lr_hbm,
    next_ref,
    chip_ref,
    current_ref,
    zscores_ref,
    ridge_ref,
    band_ref,
    back_ref,
    back_other_ref,
    lr_ref,
    sems,
):
    me, core = lax.axis_index("row"), lax.axis_index("col")
    blocks, width, tile, _ = band_ref.shape
    rows = blocks * tile
    reach = width // 2
    mine = pl.ds(pl.multiple_of(core * rows, rows), rows)
    other = pl.ds(pl.multiple_of((1 - core) * rows, rows), rows)
    copies = fetch(
        [
            (mine_hbm, chip_ref.at[mine]),
            (other_hbm, chip_ref.at[other]),
            (band_hbm, band_ref),
            (current_hbm, current_ref),
            (zscores_hbm, zscores_ref),
            (ridge_hbm, ridge_ref),
            (back_hbm, back_ref),
            (back_other_hbm, back_other_ref),
            (lr_hbm, lr_ref),
        ],
        sems,
    )
    for copy in copies[:3]:
        copy.wait()

    def product(b, at):
        low, high = max(0, at - reach), min(cores * blocks, at + reach + 1)
        tiles = [band_ref[b, c - at + reach] for c in range(low, high)]
        return dot(jnp.concatenate(tiles, axis=1), chip_ref[low * tile : high * tile, :])

    for n in range(cores):

        @pl.when(core == n)
        def _():
            for b in range(blocks):
                next_ref[b * tile : (b + 1) * tile, :] = product(b, n * blocks + b)

    for copy in copies[3:]:
        copy.wait()
    for b in range(blocks):
        out = slice(b * tile, (b + 1) * tile)
        current = current_ref[out, :]
        gradient = next_ref[out, :] + (ridge_ref[...] * current - zscores_ref[out, :])
        next_ref[out, :] = current - STEP * gradient

    for hub in range(blocks_ref.shape[0]):
        place = Place(blocks_ref[hub], blocks, cores)
        row = pl.ds(hub * tile, tile)
        own = pl.ds(pl.multiple_of(place.blk * tile, tile), tile)

        @pl.when((place.chip == me) & (place.core == core))
        def _():
            both = back_ref[row, :].astype(F32) + back_other_ref[row, :].astype(F32)
            next_ref[own, :] -= STEP * both

    for s in range(lr_ref.shape[0]):
        block = blocks_ref[hub_ref[s]]
        row = pl.ds(pl.multiple_of(local_ref[s] * tile, tile), tile)

        @pl.when(Place(block, blocks, cores).chip == me)
        def _():
            at = pl.ds(pl.multiple_of((block - me * (cores * blocks)) * tile, tile), tile)
            next_ref[row, :] -= STEP * dot(lr_ref[s], chip_ref[at, :])


def edge_kernel(
    outer_hbm, band_hbm, partial_hbm, out_hbm, outer_ref, band_ref, partial_ref, out_ref, sems
):
    core = lax.axis_index("col")
    blocks, reach, tile, _ = band_ref.shape
    first = (band_hbm.shape[1] - reach) * core
    for copy in fetch(
        [
            (outer_hbm, outer_ref),
            (band_hbm.at[:, pl.ds(first, reach)], band_ref),
            (partial_hbm, partial_ref),
        ],
        sems,
    ):
        copy.wait()

    def write(b, skip, low, high):
        tiles = [band_ref[b, skip + n] for n in range(high - low)]
        out = pl.ds(b * tile, tile)
        gradient = dot(jnp.concatenate(tiles, axis=1), outer_ref[low * tile : high * tile, :])
        out_ref[out, :] = partial_ref[out, :] - STEP * gradient
        pltpu.make_async_copy(out_ref.at[out], out_hbm.at[out], sems.at[3 + b]).start()

    @pl.when(core == 0)
    def _():
        for b in range(blocks):
            write(b, 0, b, blocks)

    @pl.when(core != 0)
    def _():
        for b in range(blocks):
            write(b, blocks - 1 - b, 0, b + 1)

    for b in range(blocks):
        out = pl.ds(b * tile, tile)
        pltpu.make_async_copy(out_ref.at[out], out_hbm.at[out], sems.at[3 + b]).wait()


def step_kernel(
    cores,
    last,
    blocks_ref,
    local_ref,
    hub_ref,
    lr_ref,
    half_ref,
    half_other_ref,
    partial_hbm,
    *rest,
):
    if last:
        next_hbm, rest = rest[0], rest[1:]
    else:
        (next_hbm, panel_hbm, back_hbm, keep_ref, send_ref), rest = rest[:5], rest[5:]
    partial_ref, panel_ref, state_ref, grad_ref, term_ref, next_ref, sems = rest
    me, core = lax.axis_index("row"), lax.axis_index("col")
    count, tile, _ = lr_ref.shape
    rows = next_ref.shape[0]
    blocks = rows // tile
    hubs = blocks_ref.shape[0]
    half = half_ref.shape[0]
    copies = fetch([(partial_hbm, partial_ref)], sems)
    near = pl.ds(pl.multiple_of(core * half, half), half)
    away = pl.ds(pl.multiple_of((1 - core) * half, half), half)
    state_ref[near, :] = half_ref[...]
    state_ref[away, :] = half_other_ref[...]
    grad_ref[...] = jnp.zeros_like(grad_ref)

    for hub in range(hubs):
        place = Place(blocks_ref[hub], blocks, cores)
        own = pl.ds(pl.multiple_of(place.blk * tile, tile), tile)
        row = pl.ds(hub * tile, tile)

        @pl.when((place.chip == me) & (place.core == core))
        def _():
            grad_ref[own, :] += state_ref[row, :].astype(F32)

        @pl.when(place.chip == me)
        def _():
            state_ref[row, :] = jnp.zeros_like(state_ref[row, :])

    for s in range(count):
        col = pl.ds(pl.multiple_of(hub_ref[s] * tile, tile), tile)
        term_ref[s] = dot(lr_ref[s], state_ref[col, :])
    for s in range(count):
        grad_ref[pl.ds(pl.multiple_of(local_ref[s] * tile, tile), tile), :] += term_ref[s]

    for copy in copies:
        copy.wait()
    done = []
    for b in range(blocks):
        out = pl.ds(b * tile, tile)
        following = partial_ref[out, :] - STEP * grad_ref[out, :]
        next_ref[out, :] = following
        done += fetch([(next_ref.at[out], next_hbm.at[out])], sems.at[pl.ds(2 + b, 1)])
        if not last:
            panel_ref[out, :] = following.astype(BF16)
    if not last:
        back_ref, acc_ref = state_ref, grad_ref
        done += fetch([(panel_ref, panel_hbm)], sems.at[pl.ds(2 + blocks, 1)])
        back_terms(local_ref, hub_ref, lr_ref, panel_ref, term_ref, acc_ref, back_ref)
        done += fetch([(back_ref, back_hbm)], sems.at[pl.ds(3 + blocks, 1)])
        contributions(cores, blocks_ref, back_ref, panel_ref, keep_ref, send_ref)
    for copy in done:
        copy.wait()


def join_kernel(keep_ref, came_ref, out_ref):
    out_ref[...] = (keep_ref[...].astype(F32) + came_ref[...].astype(F32)).astype(BF16)


def shards(rows_dev, cores, effects, zscores, ridge, band, lr, lr_local, lr_hub, hub_blocks):
    blocks, _, tile, _ = band.shape
    rows, traits = effects.shape
    hubs = hub_blocks.shape[0]
    hub_rows = hubs * tile
    half = hub_rows // cores
    total = rows_dev * cores
    panel_type = jax.ShapeDtypeStruct((rows, traits), BF16)
    back_type = jax.ShapeDtypeStruct((hub_rows, traits), BF16)
    ridge = ridge[None, :]

    odd = [(i, i + 1) for i in range(cores - 1, total - 1, cores)]
    odd = odd + [(j, i) for i, j in odd]
    swap = [(0, 1), (1, 0)]

    def other_core(x):
        return lax.ppermute(x, "col", swap)

    def exchange(x):
        x = x.reshape(rows_dev, half // rows_dev, traits)
        return lax.all_to_all(x, "row", 0, 0)

    half_type = jax.ShapeDtypeStruct((half, traits), BF16)
    panels, back, keep, send = pl.pallas_call(
        functools.partial(first_kernel, cores),
        out_shape=(panel_type, back_type, half_type, half_type),
        in_specs=[HBM] * 5,
        out_specs=(VMEM,) * 4,
        scratch_shapes=[
            pltpu.VMEM((hub_rows, traits), F32),
            pltpu.SMEM(hub_blocks.shape, jnp.int32),
            pltpu.SMEM(lr_local.shape, jnp.int32),
            pltpu.SMEM(lr_hub.shape, jnp.int32),
            pltpu.VMEM(effects.shape, F32),
            pltpu.VMEM(lr.shape, BF16),
            pltpu.SemaphoreType.DMA((5,)),
            pltpu.VMEM((lr.shape[0], tile, traits), F32),
        ],
        compiler_params=FIRST,
        name="first",
    )(hub_blocks, lr_local, lr_hub, effects, lr)

    current = effects
    for sweep in range(ITERS):
        last = sweep == ITERS - 1
        outer = lax.ppermute(panels, ("row", "col"), odd)
        came = other_core(send)
        other = other_core(panels)
        back_other = other_core(back)
        chosen = pl.pallas_call(
            join_kernel,
            out_shape=half_type,
            in_specs=[VMEM] * 2,
            out_specs=VMEM,
            compiler_params=MERGE,
            name="join",
        )(keep, came)
        gathered = exchange(chosen)
        merged = pl.pallas_call(
            functools.partial(merge_kernel, cores, tile, blocks * cores),
            out_shape=jax.ShapeDtypeStruct(gathered.shape, BF16),
            in_specs=[SMEM, VMEM, ANY, ANY],
            out_specs=VMEM,
            compiler_params=MERGE,
            name="merge",
        )(hub_blocks, gathered, other, back_other)
        partial = pl.pallas_call(
            functools.partial(band_kernel, cores),
            out_shape=jax.ShapeDtypeStruct((rows, traits), F32),
            in_specs=[SMEM] * 3 + [HBM] * 9,
            out_specs=VMEM,
            scratch_shapes=[
                pltpu.VMEM((cores * rows, traits), BF16),
                pltpu.VMEM(current.shape, F32),
                pltpu.VMEM(zscores.shape, F32),
                pltpu.VMEM(ridge.shape, F32),
                pltpu.VMEM(band.shape, BF16),
                pltpu.VMEM(back.shape, BF16),
                pltpu.VMEM(back.shape, BF16),
                pltpu.VMEM(lr.shape, BF16),
                pltpu.SemaphoreType.DMA((9,)),
            ],
            compiler_params=BAND,
            cost_estimate=pl.CostEstimate(
                flops=10**6, bytes_accessed=2**20, transcendentals=0
            ),
            name="band",
        )(
            hub_blocks,
            lr_local,
            lr_hub,
            current,
            zscores,
            ridge,
            band,
            panels,
            other,
            back,
            back_other,
            lr,
        )
        partial = pl.pallas_call(
            edge_kernel,
            out_shape=jax.ShapeDtypeStruct((rows, traits), F32),
            in_specs=[HBM] * 3,
            out_specs=HBM,
            scratch_shapes=[
                pltpu.VMEM((rows, traits), BF16),
                pltpu.VMEM((blocks, band.shape[1] // 2, tile, tile), BF16),
                pltpu.VMEM((rows, traits), F32),
                pltpu.VMEM((rows, traits), F32),
                pltpu.SemaphoreType.DMA((blocks + 3,)),
            ],
            compiler_params=BAND,
            name="edge",
        )(outer, band, partial)
        mine = exchange(merged).reshape(half, traits)
        mine, partial = lax.optimization_barrier((mine, partial))
        theirs = other_core(mine)
        out_shape, out_specs = [jax.ShapeDtypeStruct((rows, traits), F32)], [HBM]
        if not last:
            out_shape += [panel_type, back_type, half_type, half_type]
            out_specs += [HBM, HBM, VMEM, VMEM]
        result = pl.pallas_call(
            functools.partial(step_kernel, cores, last),
            out_shape=tuple(out_shape),
            in_specs=[SMEM] * 3 + [VMEM] * 3 + [HBM],
            out_specs=tuple(out_specs),
            scratch_shapes=[
                pltpu.VMEM((rows, traits), F32),
                pltpu.VMEM((rows, traits), BF16),
                pltpu.VMEM((hub_rows, traits), BF16),
                pltpu.VMEM((max(rows, hub_rows), traits), F32),
                pltpu.VMEM((lr.shape[0], tile, traits), F32),
                pltpu.VMEM((rows, traits), F32),
                pltpu.SemaphoreType.DMA((blocks + 4,)),
            ],
            compiler_params=UPDATE,
            name="step",
        )(
            hub_blocks,
            lr_local,
            lr_hub,
            lr,
            mine,
            theirs,
            partial,
        )
        if last:
            return result[0]
        current, panels, back, keep, send = result


def solution(mesh):
    every = ("groups", "row", "col")
    placed = (
        P(every, None),
        P(every, None),
        P("groups"),
        P(every, None, None, None),
        P(every, None, None),
        P(every),
        P(every),
        P("groups"),
    )
    return jax.shard_map(
        functools.partial(shards, mesh.shape["row"], mesh.shape["col"]),
        mesh=mesh,
        in_specs=placed,
        out_specs=P(every, None),
        check_vma=False,
    )
```

```python
import functools

import jax
import jax.numpy as jnp
from jax import lax
from jax.experimental import pallas as pl
from jax.experimental.pallas import tpu as pltpu
from jax.sharding import PartitionSpec as P

ITERS = 2
STEP = 0.5
F32 = jnp.float32
BF16 = jnp.bfloat16
FIRST = pltpu.CompilerParams(vmem_limit_bytes=58 * 2**20)
MERGE = pltpu.CompilerParams(vmem_limit_bytes=12 * 2**20)
BAND = pltpu.CompilerParams(vmem_limit_bytes=58 * 2**20)
EDGE = pltpu.CompilerParams(vmem_limit_bytes=54500 * 2**10)
UPDATE = pltpu.CompilerParams(vmem_limit_bytes=53850 * 2**10)
VMEM = pl.BlockSpec(memory_space=pltpu.VMEM)
HBM = pl.BlockSpec(memory_space=pltpu.HBM)
ANY = pl.BlockSpec(memory_space=pl.ANY)
SMEM = pl.BlockSpec(memory_space=pltpu.SMEM)


def dot(a, b):
    return jnp.dot(a, b, preferred_element_type=F32)


def dot_t(a, b):
    return lax.dot_general(a, b, (((0,), (0,)), ((), ())), preferred_element_type=F32)


ORDERS = {8: (1, 6, 0, 2, 5, 4, 3, 7)}


def position(chip, chips):
    order = ORDERS.get(chips)
    if order is None:
        return chip
    return sum(jnp.where(chip == c, p, 0) for p, c in enumerate(order))


class Place:
    def __init__(self, block, blocks, cores):
        self.chip = block // (blocks * cores)
        self.core = (block // blocks) % cores
        self.blk = block % blocks


def back_terms(local_ref, hub_ref, lr_ref, panel_ref, term_ref, acc_ref, out_ref):
    count, tile, _ = lr_ref.shape
    for s in range(count):
        rows = pl.ds(pl.multiple_of(local_ref[s] * tile, tile), tile)
        term_ref[s] = dot_t(lr_ref[s], panel_ref[rows, :])
    acc_ref[...] = jnp.zeros_like(acc_ref)
    for s in range(count):
        acc_ref[pl.ds(pl.multiple_of(hub_ref[s] * tile, tile), tile), :] += term_ref[s]
    out_ref[...] = acc_ref[...].astype(BF16)


def fetch(pairs, sems):
    copies = [pltpu.make_async_copy(a, b, sems.at[n]) for n, (a, b) in enumerate(pairs)]
    for copy in copies:
        copy.start()
    return copies


def contributions(cores, blocks_ref, back_ref, panel_ref, keep_ref, send_ref):
    me, core = lax.axis_index("row"), lax.axis_index("col")
    hubs = blocks_ref.shape[0]
    tile = back_ref.shape[0] // hubs
    blocks = panel_ref.shape[0] // tile
    per_half = hubs // cores

    def write(ref, half):
        for j in range(per_half):
            hub = half * per_half + j
            place = Place(blocks_ref[hub], blocks, cores)
            out = pl.ds(j * tile, tile)
            row = pl.ds(pl.multiple_of(hub * tile, tile), tile)
            own = pl.ds(pl.multiple_of(place.blk * tile, tile), tile)
            here, near = place.chip == me, place.core == core

            @pl.when(jnp.logical_not(here))
            def _():
                ref[out, :] = back_ref[row, :]

            @pl.when(here & near)
            def _():
                ref[out, :] = panel_ref[own, :]

            @pl.when(here & jnp.logical_not(near))
            def _():
                ref[out, :] = jnp.zeros_like(ref[out, :])

    write(keep_ref, core)
    write(send_ref, 1 - core)


def first_kernel(cores, *refs):
    sources, (panel_ref, back_ref, keep_ref, send_ref, acc_ref) = refs[:5], refs[5:10]
    held, (sems, term_ref) = refs[10:15], refs[15:]
    for copy in fetch(list(zip(sources, held)), sems):
        copy.wait()
    blocks_ref, local_ref, hub_ref, effects_ref, lr_ref = held
    panel_ref[...] = effects_ref[...].astype(BF16)
    back_terms(local_ref, hub_ref, lr_ref, panel_ref, term_ref, acc_ref, back_ref)
    contributions(cores, blocks_ref, back_ref, panel_ref, keep_ref, send_ref)


def merge_kernel(cores, tile, per_chip, blocks_ref, in_ref, *rest):
    *_, out_ref = rest
    me, core = lax.axis_index("row"), lax.axis_index("col")
    chips, rows, _ = in_ref.shape
    hub = (core * (chips * rows) + position(me, chips) * rows) // tile
    owner = position(blocks_ref[hub] // per_chip, chips)

    def add(p, total):
        return total + jnp.where(p == owner, 0.0, in_ref[p].astype(F32))

    def put(p, carry):
        out_ref[p] = jnp.where(p == owner, total, state)
        return carry

    zero = jnp.zeros(in_ref.shape[1:], F32)
    total = lax.fori_loop(0, chips, add, zero, unroll=chips <= 16).astype(BF16)
    state = in_ref[owner]
    lax.fori_loop(0, chips, put, 0, unroll=chips <= 16)


def band_kernel(
    cores,
    blocks_ref,
    local_ref,
    hub_ref,
    current_hbm,
    zscores_hbm,
    ridge_hbm,
    band_hbm,
    mine_hbm,
    other_hbm,
    back_hbm,
    back_other_hbm,
    lr_hbm,
    next_hbm,
    chip_ref,
    current_ref,
    zscores_ref,
    ridge_ref,
    band_ref,
    back_ref,
    back_other_ref,
    lr_ref,
    next_ref,
    sems,
):
    me, core = lax.axis_index("row"), lax.axis_index("col")
    blocks, width, tile, _ = band_ref.shape
    rows = blocks * tile
    reach = width // 2
    hubs = blocks_ref.shape[0]
    mine = pl.ds(pl.multiple_of(core * rows, rows), rows)
    other = pl.ds(pl.multiple_of((1 - core) * rows, rows), rows)
    ahead = [
        (mine_hbm, chip_ref.at[mine]),
        (other_hbm, chip_ref.at[other]),
        (band_hbm, band_ref),
    ]
    behind = [
        (current_hbm, current_ref),
        (zscores_hbm, zscores_ref),
        (ridge_hbm, ridge_ref),
        (lr_hbm, lr_ref),
    ]
    extra, store = len(ahead) + len(behind), len(ahead) + len(behind) + 2 * hubs
    early = fetch(ahead, sems)
    late = fetch(behind, sems.at[pl.ds(len(ahead), len(behind))])

    def owned(hub):
        place = Place(blocks_ref[hub], blocks, cores)
        return (place.chip == me) & (place.core == core), place.blk

    def sums(hub):
        row = pl.ds(hub * tile, tile)
        return [
            pltpu.make_async_copy(back_hbm.at[row], back_ref.at[row], sems.at[extra + 2 * hub]),
            pltpu.make_async_copy(
                back_other_hbm.at[row], back_other_ref.at[row], sems.at[extra + 2 * hub + 1]
            ),
        ]

    for hub in range(hubs):

        @pl.when(owned(hub)[0])
        def _():
            for copy in sums(hub):
                copy.start()

    for copy in early:
        copy.wait()

    def product(b, at):
        low, high = max(0, at - reach), min(cores * blocks, at + reach + 1)
        tiles = [band_ref[b, c - at + reach] for c in range(low, high)]
        return dot(jnp.concatenate(tiles, axis=1), chip_ref[low * tile : high * tile, :])

    for n in range(cores):

        @pl.when(core == n)
        def _():
            for b in range(blocks):
                next_ref[b * tile : (b + 1) * tile, :] = product(b, n * blocks + b)

    for copy in late:
        copy.wait()
    for b in range(blocks):
        out = slice(b * tile, (b + 1) * tile)
        current = current_ref[out, :]
        gradient = next_ref[out, :] + (ridge_ref[...] * current - zscores_ref[out, :])
        next_ref[out, :] = current - STEP * gradient

    for hub in range(hubs):
        here, blk = owned(hub)
        row = pl.ds(hub * tile, tile)
        own = pl.ds(pl.multiple_of(blk * tile, tile), tile)

        @pl.when(here)
        def _():
            for copy in sums(hub):
                copy.wait()
            both = back_ref[row, :].astype(F32) + back_other_ref[row, :].astype(F32)
            next_ref[own, :] -= STEP * both

    for s in range(lr_ref.shape[0]):
        block = blocks_ref[hub_ref[s]]
        row = pl.ds(pl.multiple_of(local_ref[s] * tile, tile), tile)

        @pl.when(Place(block, blocks, cores).chip == me)
        def _():
            at = pl.ds(pl.multiple_of((block - me * (cores * blocks)) * tile, tile), tile)
            next_ref[row, :] -= STEP * dot(lr_ref[s], chip_ref[at, :])

    done = pltpu.make_async_copy(next_ref, next_hbm, sems.at[store])
    done.start()
    done.wait()


def edge_kernel(
    outer_ref, band_hbm, partial_hbm, out_hbm, band_ref, partial_ref, out_ref, sems
):
    core = lax.axis_index("col")
    blocks, reach, tile, _ = band_ref.shape
    first = (band_hbm.shape[1] - reach) * core
    for copy in fetch(
        [
            (band_hbm.at[:, pl.ds(first, reach)], band_ref),
            (partial_hbm, partial_ref),
        ],
        sems,
    ):
        copy.wait()

    def write(b, skip, low, high):
        tiles = [band_ref[b, skip + n] for n in range(high - low)]
        out = pl.ds(b * tile, tile)
        gradient = dot(jnp.concatenate(tiles, axis=1), outer_ref[low * tile : high * tile, :])
        out_ref[out, :] = partial_ref[out, :] - STEP * gradient
        pltpu.make_async_copy(out_ref.at[out], out_hbm.at[out], sems.at[3 + b]).start()

    @pl.when(core == 0)
    def _():
        for b in range(blocks):
            write(b, 0, b, blocks)

    @pl.when(core != 0)
    def _():
        for b in range(blocks):
            write(b, blocks - 1 - b, 0, b + 1)

    for b in range(blocks):
        out = pl.ds(b * tile, tile)
        pltpu.make_async_copy(out_ref.at[out], out_hbm.at[out], sems.at[3 + b]).wait()


def step_kernel(
    cores,
    last,
    blocks_ref,
    local_ref,
    hub_ref,
    lr_ref,
    half_ref,
    half_other_ref,
    partial_hbm,
    *rest,
):
    if last:
        next_hbm, rest = rest[0], rest[1:]
    else:
        (next_hbm, panel_hbm, back_hbm, keep_ref, send_ref), rest = rest[:5], rest[5:]
    partial_ref, panel_ref, state_ref, grad_ref, term_ref, next_ref, sems = rest
    me, core = lax.axis_index("row"), lax.axis_index("col")
    count, tile, _ = lr_ref.shape
    rows = next_ref.shape[0]
    blocks = rows // tile
    hubs = blocks_ref.shape[0]
    half = half_ref.shape[0]
    copies = fetch([(partial_hbm, partial_ref)], sems)
    near = pl.ds(pl.multiple_of(core * half, half), half)
    away = pl.ds(pl.multiple_of((1 - core) * half, half), half)
    state_ref[near, :] = half_ref[...]
    state_ref[away, :] = half_other_ref[...]
    grad_ref[...] = jnp.zeros_like(grad_ref)

    for hub in range(hubs):
        place = Place(blocks_ref[hub], blocks, cores)
        own = pl.ds(pl.multiple_of(place.blk * tile, tile), tile)
        row = pl.ds(hub * tile, tile)

        @pl.when((place.chip == me) & (place.core == core))
        def _():
            grad_ref[own, :] += state_ref[row, :].astype(F32)

        @pl.when(place.chip == me)
        def _():
            state_ref[row, :] = jnp.zeros_like(state_ref[row, :])

    for s in range(count):
        col = pl.ds(pl.multiple_of(hub_ref[s] * tile, tile), tile)
        term_ref[s] = dot(lr_ref[s], state_ref[col, :])
    for s in range(count):
        grad_ref[pl.ds(pl.multiple_of(local_ref[s] * tile, tile), tile), :] += term_ref[s]

    for copy in copies:
        copy.wait()
    done = []
    for b in range(blocks):
        out = pl.ds(b * tile, tile)
        following = partial_ref[out, :] - STEP * grad_ref[out, :]
        next_ref[out, :] = following
        done += fetch([(next_ref.at[out], next_hbm.at[out])], sems.at[pl.ds(2 + b, 1)])
        if not last:
            panel_ref[out, :] = following.astype(BF16)
    if not last:
        back_ref, acc_ref = state_ref, grad_ref
        done += fetch([(panel_ref, panel_hbm)], sems.at[pl.ds(2 + blocks, 1)])
        back_terms(local_ref, hub_ref, lr_ref, panel_ref, term_ref, acc_ref, back_ref)
        done += fetch([(back_ref, back_hbm)], sems.at[pl.ds(3 + blocks, 1)])
        contributions(cores, blocks_ref, back_ref, panel_ref, keep_ref, send_ref)
    for copy in done:
        copy.wait()


def join_kernel(keep_ref, came_ref, out_ref):
    out_ref[...] = (keep_ref[...].astype(F32) + came_ref[...].astype(F32)).astype(BF16)


def shards(rows_dev, cores, effects, zscores, ridge, band, lr, lr_local, lr_hub, hub_blocks):
    blocks, _, tile, _ = band.shape
    rows, traits = effects.shape
    hubs = hub_blocks.shape[0]
    hub_rows = hubs * tile
    half = hub_rows // cores
    total = rows_dev * cores
    panel_type = jax.ShapeDtypeStruct((rows, traits), BF16)
    back_type = jax.ShapeDtypeStruct((hub_rows, traits), BF16)
    ridge = ridge[None, :]

    odd = [(i, i + 1) for i in range(cores - 1, total - 1, cores)]
    odd = odd + [(j, i) for i, j in odd]
    swap = [(0, 1), (1, 0)]

    def other_core(x):
        return lax.ppermute(x, "col", swap)

    def exchange(x):
        x = x.reshape(rows_dev, half // rows_dev, traits)
        order = ORDERS.get(rows_dev)
        return lax.all_to_all(x, "row", 0, 0, axis_index_groups=order and [list(order)])

    half_type = jax.ShapeDtypeStruct((half, traits), BF16)
    panels, back, keep, send = pl.pallas_call(
        functools.partial(first_kernel, cores),
        out_shape=(panel_type, back_type, half_type, half_type),
        in_specs=[HBM] * 5,
        out_specs=(VMEM,) * 4,
        scratch_shapes=[
            pltpu.VMEM((hub_rows, traits), F32),
            pltpu.SMEM(hub_blocks.shape, jnp.int32),
            pltpu.SMEM(lr_local.shape, jnp.int32),
            pltpu.SMEM(lr_hub.shape, jnp.int32),
            pltpu.VMEM(effects.shape, F32),
            pltpu.VMEM(lr.shape, BF16),
            pltpu.SemaphoreType.DMA((5,)),
            pltpu.VMEM((lr.shape[0], tile, traits), F32),
        ],
        compiler_params=FIRST,
        name="first",
    )(hub_blocks, lr_local, lr_hub, effects, lr)

    current = effects
    for sweep in range(ITERS):
        last = sweep == ITERS - 1
        outer = lax.ppermute(panels, ("row", "col"), odd)
        came = other_core(send)
        other = other_core(panels)
        back_other = other_core(back)
        chosen = pl.pallas_call(
            join_kernel,
            out_shape=half_type,
            in_specs=[VMEM] * 2,
            out_specs=VMEM,
            compiler_params=MERGE,
            name="join",
        )(keep, came)
        gathered = exchange(chosen)
        merged = pl.pallas_call(
            functools.partial(merge_kernel, cores, tile, blocks * cores),
            out_shape=jax.ShapeDtypeStruct(gathered.shape, BF16),
            in_specs=[SMEM, VMEM, ANY, ANY],
            out_specs=VMEM,
            compiler_params=MERGE,
            name="merge",
        )(hub_blocks, gathered, other, back_other)
        partial = pl.pallas_call(
            functools.partial(band_kernel, cores),
            out_shape=jax.ShapeDtypeStruct((rows, traits), F32),
            in_specs=[SMEM] * 3 + [HBM] * 9,
            out_specs=HBM,
            scratch_shapes=[
                pltpu.VMEM((cores * rows, traits), BF16),
                pltpu.VMEM(current.shape, F32),
                pltpu.VMEM(zscores.shape, F32),
                pltpu.VMEM(ridge.shape, F32),
                pltpu.VMEM(band.shape, BF16),
                pltpu.VMEM(back.shape, BF16),
                pltpu.VMEM(back.shape, BF16),
                pltpu.VMEM(lr.shape, BF16),
                pltpu.VMEM((rows, traits), F32),
                pltpu.SemaphoreType.DMA((8 + 2 * hubs,)),
            ],
            compiler_params=BAND,
            cost_estimate=pl.CostEstimate(
                flops=10**6, bytes_accessed=2**20, transcendentals=0
            ),
            name="band",
        )(
            hub_blocks,
            lr_local,
            lr_hub,
            current,
            zscores,
            ridge,
            band,
            panels,
            other,
            back,
            back_other,
            lr,
        )
        partial = pl.pallas_call(
            edge_kernel,
            out_shape=jax.ShapeDtypeStruct((rows, traits), F32),
            in_specs=[VMEM, HBM, HBM],
            out_specs=HBM,
            scratch_shapes=[
                pltpu.VMEM((blocks, band.shape[1] // 2, tile, tile), BF16),
                pltpu.VMEM((rows, traits), F32),
                pltpu.VMEM((rows, traits), F32),
                pltpu.SemaphoreType.DMA((blocks + 3,)),
            ],
            compiler_params=EDGE,
            name="edge",
        )(outer, band, partial)
        mine = exchange(merged).reshape(half, traits)
        mine, partial = lax.optimization_barrier((mine, partial))
        theirs = other_core(mine)
        out_shape, out_specs = [jax.ShapeDtypeStruct((rows, traits), F32)], [HBM]
        if not last:
            out_shape += [panel_type, back_type, half_type, half_type]
            out_specs += [HBM, HBM, VMEM, VMEM]
        result = pl.pallas_call(
            functools.partial(step_kernel, cores, last),
            out_shape=tuple(out_shape),
            in_specs=[SMEM] * 3 + [VMEM] * 3 + [HBM],
            out_specs=tuple(out_specs),
            scratch_shapes=[
                pltpu.VMEM((rows, traits), F32),
                pltpu.VMEM((rows, traits), BF16),
                pltpu.VMEM((hub_rows, traits), BF16),
                pltpu.VMEM((max(rows, hub_rows), traits), F32),
                pltpu.VMEM((lr.shape[0], tile, traits), F32),
                pltpu.VMEM((rows, traits), F32),
                pltpu.SemaphoreType.DMA((blocks + 4,)),
            ],
            compiler_params=UPDATE,
            name="step",
        )(
            hub_blocks,
            lr_local,
            lr_hub,
            lr,
            mine,
            theirs,
            partial,
        )
        if last:
            return result[0]
        current, panels, back, keep, send = result


def solution(mesh):
    every = ("groups", "row", "col")
    placed = (
        P(every, None),
        P(every, None),
        P("groups"),
        P(every, None, None, None),
        P(every, None, None),
        P(every),
        P(every),
        P("groups"),
    )
    return jax.shard_map(
        functools.partial(shards, mesh.shape["row"], mesh.shape["col"]),
        mesh=mesh,
        in_specs=placed,
        out_specs=P(every, None),
        check_vma=False,
    )
```

```python
import functools

import jax
import jax.numpy as jnp
from jax import lax
from jax.experimental import pallas as pl
from jax.experimental.pallas import tpu as pltpu
from jax.sharding import PartitionSpec as P

ITERS = 2
STEP = 0.5
F32 = jnp.float32
BF16 = jnp.bfloat16
FIRST = pltpu.CompilerParams(vmem_limit_bytes=58 * 2**20)
MERGE = pltpu.CompilerParams(vmem_limit_bytes=12 * 2**20)
BAND = pltpu.CompilerParams(vmem_limit_bytes=58 * 2**20)
EDGE = pltpu.CompilerParams(vmem_limit_bytes=54500 * 2**10)
UPDATE = pltpu.CompilerParams(vmem_limit_bytes=53850 * 2**10)
VMEM = pl.BlockSpec(memory_space=pltpu.VMEM)
HBM = pl.BlockSpec(memory_space=pltpu.HBM)
ANY = pl.BlockSpec(memory_space=pl.ANY)
SMEM = pl.BlockSpec(memory_space=pltpu.SMEM)


def dot(a, b):
    return jnp.dot(a, b, preferred_element_type=F32)


def dot_t(a, b):
    return lax.dot_general(a, b, (((0,), (0,)), ((), ())), preferred_element_type=F32)


ORDERS = {8: (4, 6, 1, 5, 0, 2, 7, 3)}


def position(chip, chips):
    order = ORDERS.get(chips)
    if order is None:
        return chip
    return sum(jnp.where(chip == c, p, 0) for p, c in enumerate(order))


class Place:
    def __init__(self, block, blocks, cores):
        self.chip = block // (blocks * cores)
        self.core = (block // blocks) % cores
        self.blk = block % blocks


def back_terms(local_ref, hub_ref, lr_ref, panel_ref, term_ref, acc_ref, out_ref):
    count, tile, _ = lr_ref.shape
    for s in range(count):
        rows = pl.ds(pl.multiple_of(local_ref[s] * tile, tile), tile)
        term_ref[s] = dot_t(lr_ref[s], panel_ref[rows, :])
    acc_ref[...] = jnp.zeros_like(acc_ref)
    for s in range(count):
        acc_ref[pl.ds(pl.multiple_of(hub_ref[s] * tile, tile), tile), :] += term_ref[s]
    out_ref[...] = acc_ref[...].astype(BF16)


def fetch(pairs, sems):
    copies = [pltpu.make_async_copy(a, b, sems.at[n]) for n, (a, b) in enumerate(pairs)]
    for copy in copies:
        copy.start()
    return copies


def contributions(cores, blocks_ref, back_ref, panel_ref, keep_ref, send_ref):
    me, core = lax.axis_index("row"), lax.axis_index("col")
    hubs = blocks_ref.shape[0]
    tile = back_ref.shape[0] // hubs
    blocks = panel_ref.shape[0] // tile
    per_half = hubs // cores

    def write(ref, half):
        for j in range(per_half):
            hub = half * per_half + j
            place = Place(blocks_ref[hub], blocks, cores)
            out = pl.ds(j * tile, tile)
            row = pl.ds(pl.multiple_of(hub * tile, tile), tile)
            own = pl.ds(pl.multiple_of(place.blk * tile, tile), tile)
            here, near = place.chip == me, place.core == core

            @pl.when(jnp.logical_not(here))
            def _():
                ref[out, :] = back_ref[row, :]

            @pl.when(here & near)
            def _():
                ref[out, :] = panel_ref[own, :]

            @pl.when(here & jnp.logical_not(near))
            def _():
                ref[out, :] = jnp.zeros_like(ref[out, :])

    write(keep_ref, core)
    write(send_ref, 1 - core)


def first_kernel(cores, *refs):
    sources, (panel_ref, back_ref, keep_ref, send_ref, acc_ref) = refs[:5], refs[5:10]
    held, (sems, term_ref) = refs[10:15], refs[15:]
    for copy in fetch(list(zip(sources, held)), sems):
        copy.wait()
    blocks_ref, local_ref, hub_ref, effects_ref, lr_ref = held
    panel_ref[...] = effects_ref[...].astype(BF16)
    back_terms(local_ref, hub_ref, lr_ref, panel_ref, term_ref, acc_ref, back_ref)
    contributions(cores, blocks_ref, back_ref, panel_ref, keep_ref, send_ref)


def merge_kernel(cores, tile, per_chip, blocks_ref, in_ref, *rest):
    *_, out_ref = rest
    me, core = lax.axis_index("row"), lax.axis_index("col")
    chips, rows, _ = in_ref.shape
    hub = (core * (chips * rows) + position(me, chips) * rows) // tile
    owner = position(blocks_ref[hub] // per_chip, chips)

    def add(p, total):
        return total + jnp.where(p == owner, 0.0, in_ref[p].astype(F32))

    def put(p, carry):
        out_ref[p] = jnp.where(p == owner, total, state)
        return carry

    zero = jnp.zeros(in_ref.shape[1:], F32)
    total = lax.fori_loop(0, chips, add, zero, unroll=chips <= 16).astype(BF16)
    state = in_ref[owner]
    lax.fori_loop(0, chips, put, 0, unroll=chips <= 16)


def band_kernel(
    cores,
    blocks_ref,
    local_ref,
    hub_ref,
    current_hbm,
    zscores_hbm,
    ridge_hbm,
    band_hbm,
    mine_hbm,
    other_hbm,
    back_hbm,
    back_other_hbm,
    lr_hbm,
    next_hbm,
    chip_ref,
    current_ref,
    zscores_ref,
    ridge_ref,
    band_ref,
    back_ref,
    back_other_ref,
    lr_ref,
    next_ref,
    sems,
):
    me, core = lax.axis_index("row"), lax.axis_index("col")
    blocks, width, tile, _ = band_ref.shape
    rows = blocks * tile
    reach = width // 2
    hubs = blocks_ref.shape[0]
    mine = pl.ds(pl.multiple_of(core * rows, rows), rows)
    other = pl.ds(pl.multiple_of((1 - core) * rows, rows), rows)
    ahead = [
        (mine_hbm, chip_ref.at[mine]),
        (other_hbm, chip_ref.at[other]),
        (band_hbm, band_ref),
    ]
    behind = [
        (current_hbm, current_ref),
        (zscores_hbm, zscores_ref),
        (ridge_hbm, ridge_ref),
        (lr_hbm, lr_ref),
    ]
    extra, store = len(ahead) + len(behind), len(ahead) + len(behind) + 2 * hubs
    early = fetch(ahead, sems)
    late = fetch(behind, sems.at[pl.ds(len(ahead), len(behind))])

    def owned(hub):
        place = Place(blocks_ref[hub], blocks, cores)
        return (place.chip == me) & (place.core == core), place.blk

    def sums(hub):
        row = pl.ds(hub * tile, tile)
        return [
            pltpu.make_async_copy(back_hbm.at[row], back_ref.at[row], sems.at[extra + 2 * hub]),
            pltpu.make_async_copy(
                back_other_hbm.at[row], back_other_ref.at[row], sems.at[extra + 2 * hub + 1]
            ),
        ]

    for hub in range(hubs):

        @pl.when(owned(hub)[0])
        def _():
            for copy in sums(hub):
                copy.start()

    for copy in early:
        copy.wait()

    def product(b, at):
        low, high = max(0, at - reach), min(cores * blocks, at + reach + 1)
        tiles = [band_ref[b, c - at + reach] for c in range(low, high)]
        return dot(jnp.concatenate(tiles, axis=1), chip_ref[low * tile : high * tile, :])

    for n in range(cores):

        @pl.when(core == n)
        def _():
            for b in range(blocks):
                next_ref[b * tile : (b + 1) * tile, :] = product(b, n * blocks + b)

    for copy in late:
        copy.wait()
    for b in range(blocks):
        out = slice(b * tile, (b + 1) * tile)
        current = current_ref[out, :]
        gradient = next_ref[out, :] + (ridge_ref[...] * current - zscores_ref[out, :])
        next_ref[out, :] = current - STEP * gradient

    for hub in range(hubs):
        here, blk = owned(hub)
        row = pl.ds(hub * tile, tile)
        own = pl.ds(pl.multiple_of(blk * tile, tile), tile)

        @pl.when(here)
        def _():
            for copy in sums(hub):
                copy.wait()
            both = back_ref[row, :].astype(F32) + back_other_ref[row, :].astype(F32)
            next_ref[own, :] -= STEP * both

    for s in range(lr_ref.shape[0]):
        block = blocks_ref[hub_ref[s]]
        row = pl.ds(pl.multiple_of(local_ref[s] * tile, tile), tile)

        @pl.when(Place(block, blocks, cores).chip == me)
        def _():
            at = pl.ds(pl.multiple_of((block - me * (cores * blocks)) * tile, tile), tile)
            next_ref[row, :] -= STEP * dot(lr_ref[s], chip_ref[at, :])

    done = pltpu.make_async_copy(next_ref, next_hbm, sems.at[store])
    done.start()
    done.wait()


def step_kernel(
    cores,
    last,
    blocks_ref,
    local_ref,
    hub_ref,
    lr_ref,
    half_ref,
    half_other_ref,
    partial_hbm,
    outer_hbm,
    band_hbm,
    *rest,
):
    if last:
        next_hbm, rest = rest[0], rest[1:]
    else:
        (next_hbm, panel_hbm, back_hbm, keep_ref, send_ref), rest = rest[:5], rest[5:]
    partial_ref, panel_ref, state_ref, grad_ref, term_ref, next_ref, edge_ref, sems = rest
    me, core = lax.axis_index("row"), lax.axis_index("col")
    count, tile, _ = lr_ref.shape
    rows = next_ref.shape[0]
    blocks = rows // tile
    hubs = blocks_ref.shape[0]
    half = half_ref.shape[0]
    reach = edge_ref.shape[1]
    first_edge = (band_hbm.shape[1] - reach) * core
    copies = fetch(
        [
            (outer_hbm, panel_ref),
            (band_hbm.at[:, pl.ds(first_edge, reach)], edge_ref),
            (partial_hbm, partial_ref),
        ],
        sems,
    )
    near = pl.ds(pl.multiple_of(core * half, half), half)
    away = pl.ds(pl.multiple_of((1 - core) * half, half), half)
    state_ref[near, :] = half_ref[...]
    state_ref[away, :] = half_other_ref[...]

    def edge(b, skip, low, high):
        tiles = [edge_ref[b, skip + n] for n in range(high - low)]
        return dot(jnp.concatenate(tiles, axis=1), panel_ref[low * tile : high * tile, :])

    copies[0].wait()
    copies[1].wait()

    @pl.when(core == 0)
    def _():
        for b in range(blocks):
            grad_ref[b * tile : (b + 1) * tile, :] = edge(b, 0, b, blocks)

    @pl.when(core != 0)
    def _():
        for b in range(blocks):
            grad_ref[b * tile : (b + 1) * tile, :] = edge(b, blocks - 1 - b, 0, b + 1)

    for hub in range(hubs):
        place = Place(blocks_ref[hub], blocks, cores)
        own = pl.ds(pl.multiple_of(place.blk * tile, tile), tile)
        row = pl.ds(hub * tile, tile)

        @pl.when((place.chip == me) & (place.core == core))
        def _():
            grad_ref[own, :] += state_ref[row, :].astype(F32)

        @pl.when(place.chip == me)
        def _():
            state_ref[row, :] = jnp.zeros_like(state_ref[row, :])

    for s in range(count):
        col = pl.ds(pl.multiple_of(hub_ref[s] * tile, tile), tile)
        term_ref[s] = dot(lr_ref[s], state_ref[col, :])
    for s in range(count):
        grad_ref[pl.ds(pl.multiple_of(local_ref[s] * tile, tile), tile), :] += term_ref[s]

    copies[2].wait()
    done = []
    for b in range(blocks):
        out = pl.ds(b * tile, tile)
        following = partial_ref[out, :] - STEP * grad_ref[out, :]
        next_ref[out, :] = following
        done += fetch([(next_ref.at[out], next_hbm.at[out])], sems.at[pl.ds(3 + b, 1)])
        if not last:
            panel_ref[out, :] = following.astype(BF16)
    if not last:
        back_ref, acc_ref = state_ref, grad_ref
        done += fetch([(panel_ref, panel_hbm)], sems.at[pl.ds(3 + blocks, 1)])
        back_terms(local_ref, hub_ref, lr_ref, panel_ref, term_ref, acc_ref, back_ref)
        done += fetch([(back_ref, back_hbm)], sems.at[pl.ds(4 + blocks, 1)])
        contributions(cores, blocks_ref, back_ref, panel_ref, keep_ref, send_ref)
    for copy in done:
        copy.wait()


def join_kernel(keep_ref, came_ref, out_ref):
    out_ref[...] = (keep_ref[...].astype(F32) + came_ref[...].astype(F32)).astype(BF16)


def shards(rows_dev, cores, effects, zscores, ridge, band, lr, lr_local, lr_hub, hub_blocks):
    blocks, _, tile, _ = band.shape
    rows, traits = effects.shape
    hubs = hub_blocks.shape[0]
    hub_rows = hubs * tile
    half = hub_rows // cores
    total = rows_dev * cores
    panel_type = jax.ShapeDtypeStruct((rows, traits), BF16)
    back_type = jax.ShapeDtypeStruct((hub_rows, traits), BF16)
    ridge = ridge[None, :]

    odd = [(i, i + 1) for i in range(cores - 1, total - 1, cores)]
    odd = odd + [(j, i) for i, j in odd]
    swap = [(0, 1), (1, 0)]

    def other_core(x):
        return lax.ppermute(x, "col", swap)

    def exchange(x):
        x = x.reshape(rows_dev, half // rows_dev, traits)
        order = ORDERS.get(rows_dev)
        return lax.all_to_all(x, "row", 0, 0, axis_index_groups=order and [list(order)])

    half_type = jax.ShapeDtypeStruct((half, traits), BF16)
    panels, back, keep, send = pl.pallas_call(
        functools.partial(first_kernel, cores),
        out_shape=(panel_type, back_type, half_type, half_type),
        in_specs=[HBM] * 5,
        out_specs=(VMEM,) * 4,
        scratch_shapes=[
            pltpu.VMEM((hub_rows, traits), F32),
            pltpu.SMEM(hub_blocks.shape, jnp.int32),
            pltpu.SMEM(lr_local.shape, jnp.int32),
            pltpu.SMEM(lr_hub.shape, jnp.int32),
            pltpu.VMEM(effects.shape, F32),
            pltpu.VMEM(lr.shape, BF16),
            pltpu.SemaphoreType.DMA((5,)),
            pltpu.VMEM((lr.shape[0], tile, traits), F32),
        ],
        compiler_params=FIRST,
        name="first",
    )(hub_blocks, lr_local, lr_hub, effects, lr)

    current = effects
    for sweep in range(ITERS):
        last = sweep == ITERS - 1
        outer = lax.ppermute(panels, ("row", "col"), odd)
        came = other_core(send)
        other = other_core(panels)
        back_other = other_core(back)
        chosen = pl.pallas_call(
            join_kernel,
            out_shape=half_type,
            in_specs=[VMEM] * 2,
            out_specs=VMEM,
            compiler_params=MERGE,
            name="join",
        )(keep, came)
        gathered = exchange(chosen)
        merged = pl.pallas_call(
            functools.partial(merge_kernel, cores, tile, blocks * cores),
            out_shape=jax.ShapeDtypeStruct(gathered.shape, BF16),
            in_specs=[SMEM, VMEM, ANY, ANY],
            out_specs=VMEM,
            compiler_params=MERGE,
            name="merge",
        )(hub_blocks, gathered, other, back_other)
        partial = pl.pallas_call(
            functools.partial(band_kernel, cores),
            out_shape=jax.ShapeDtypeStruct((rows, traits), F32),
            in_specs=[SMEM] * 3 + [HBM] * 9,
            out_specs=HBM,
            scratch_shapes=[
                pltpu.VMEM((cores * rows, traits), BF16),
                pltpu.VMEM(current.shape, F32),
                pltpu.VMEM(zscores.shape, F32),
                pltpu.VMEM(ridge.shape, F32),
                pltpu.VMEM(band.shape, BF16),
                pltpu.VMEM(back.shape, BF16),
                pltpu.VMEM(back.shape, BF16),
                pltpu.VMEM(lr.shape, BF16),
                pltpu.VMEM((rows, traits), F32),
                pltpu.SemaphoreType.DMA((8 + 2 * hubs,)),
            ],
            compiler_params=BAND,
            cost_estimate=pl.CostEstimate(
                flops=10**6, bytes_accessed=2**20, transcendentals=0
            ),
            name="band",
        )(
            hub_blocks,
            lr_local,
            lr_hub,
            current,
            zscores,
            ridge,
            band,
            panels,
            other,
            back,
            back_other,
            lr,
        )
        mine = exchange(merged).reshape(half, traits)
        mine, partial, outer = lax.optimization_barrier((mine, partial, outer))
        theirs = other_core(mine)
        out_shape, out_specs = [jax.ShapeDtypeStruct((rows, traits), F32)], [HBM]
        if not last:
            out_shape += [panel_type, back_type, half_type, half_type]
            out_specs += [HBM, HBM, VMEM, VMEM]
        result = pl.pallas_call(
            functools.partial(step_kernel, cores, last),
            out_shape=tuple(out_shape),
            in_specs=[SMEM] * 3 + [VMEM] * 3 + [HBM] * 3,
            out_specs=tuple(out_specs),
            scratch_shapes=[
                pltpu.VMEM((rows, traits), F32),
                pltpu.VMEM((rows, traits), BF16),
                pltpu.VMEM((hub_rows, traits), BF16),
                pltpu.VMEM((max(rows, hub_rows), traits), F32),
                pltpu.VMEM((lr.shape[0], tile, traits), F32),
                pltpu.VMEM((rows, traits), F32),
                pltpu.VMEM((blocks, band.shape[1] // 2, tile, tile), BF16),
                pltpu.SemaphoreType.DMA((blocks + 5,)),
            ],
            compiler_params=UPDATE,
            name="step",
        )(
            hub_blocks,
            lr_local,
            lr_hub,
            lr,
            mine,
            theirs,
            partial,
            outer,
            band,
        )
        if last:
            return result[0]
        current, panels, back, keep, send = result


def solution(mesh):
    every = ("groups", "row", "col")
    placed = (
        P(every, None),
        P(every, None),
        P("groups"),
        P(every, None, None, None),
        P(every, None, None),
        P(every),
        P(every),
        P("groups"),
    )
    return jax.shard_map(
        functools.partial(shards, mesh.shape["row"], mesh.shape["col"]),
        mesh=mesh,
        in_specs=placed,
        out_specs=P(every, None),
        check_vma=False,
    )
```

```python
import functools

import jax
import jax.numpy as jnp
from jax import lax
from jax.experimental import pallas as pl
from jax.experimental.pallas import tpu as pltpu
from jax.sharding import PartitionSpec as P

ITERS = 2
STEP = 0.5
F32 = jnp.float32
BF16 = jnp.bfloat16
FIRST = pltpu.CompilerParams(vmem_limit_bytes=58 * 2**20)
MERGE = pltpu.CompilerParams(vmem_limit_bytes=12 * 2**20)
BAND = pltpu.CompilerParams(vmem_limit_bytes=58 * 2**20)
EDGE = pltpu.CompilerParams(vmem_limit_bytes=54500 * 2**10)
UPDATE = pltpu.CompilerParams(vmem_limit_bytes=53850 * 2**10)
VMEM = pl.BlockSpec(memory_space=pltpu.VMEM)
HBM = pl.BlockSpec(memory_space=pltpu.HBM)
ANY = pl.BlockSpec(memory_space=pl.ANY)
SMEM = pl.BlockSpec(memory_space=pltpu.SMEM)


def dot(a, b):
    return jnp.dot(a, b, preferred_element_type=F32)


def dot_t(a, b):
    return lax.dot_general(a, b, (((0,), (0,)), ((), ())), preferred_element_type=F32)


ORDERS = {8: (3, 6, 1, 0, 7, 5, 4, 2)}


def position(chip, chips):
    order = ORDERS.get(chips)
    if order is None:
        return chip
    return sum(jnp.where(chip == c, p, 0) for p, c in enumerate(order))


class Place:
    def __init__(self, block, blocks, cores):
        self.chip = block // (blocks * cores)
        self.core = (block // blocks) % cores
        self.blk = block % blocks


def back_terms(local_ref, hub_ref, lr_ref, panel_ref, term_ref, acc_ref, out_ref):
    count, tile, _ = lr_ref.shape
    for s in range(count):
        rows = pl.ds(pl.multiple_of(local_ref[s] * tile, tile), tile)
        term_ref[s] = dot_t(lr_ref[s], panel_ref[rows, :])
    acc_ref[...] = jnp.zeros_like(acc_ref)
    for s in range(count):
        acc_ref[pl.ds(pl.multiple_of(hub_ref[s] * tile, tile), tile), :] += term_ref[s]
    out_ref[...] = acc_ref[...].astype(BF16)


def fetch(pairs, sems):
    copies = [pltpu.make_async_copy(a, b, sems.at[n]) for n, (a, b) in enumerate(pairs)]
    for copy in copies:
        copy.start()
    return copies


def contributions(cores, blocks_ref, back_ref, panel_ref, keep_ref, send_ref):
    me, core = lax.axis_index("row"), lax.axis_index("col")
    hubs = blocks_ref.shape[0]
    tile = back_ref.shape[0] // hubs
    blocks = panel_ref.shape[0] // tile
    per_half = hubs // cores

    def write(ref, half):
        for j in range(per_half):
            hub = half * per_half + j
            place = Place(blocks_ref[hub], blocks, cores)
            out = pl.ds(j * tile, tile)
            row = pl.ds(pl.multiple_of(hub * tile, tile), tile)
            own = pl.ds(pl.multiple_of(place.blk * tile, tile), tile)
            here, near = place.chip == me, place.core == core

            @pl.when(jnp.logical_not(here))
            def _():
                ref[out, :] = back_ref[row, :]

            @pl.when(here & near)
            def _():
                ref[out, :] = panel_ref[own, :]

            @pl.when(here & jnp.logical_not(near))
            def _():
                ref[out, :] = jnp.zeros_like(ref[out, :])

    write(keep_ref, core)
    write(send_ref, 1 - core)


def first_kernel(cores, *refs):
    sources, outs, acc_ref = refs[:5], refs[5:9], refs[9]
    held, (sems, term_ref) = refs[10:15], refs[15:17]
    panel_ref, back_ref, keep_ref, send_ref = refs[17:21]
    for copy in fetch(list(zip(sources, held)), sems):
        copy.wait()
    blocks_ref, local_ref, hub_ref, effects_ref, lr_ref = held
    panel_ref[...] = effects_ref[...].astype(BF16)
    done = fetch([(panel_ref, outs[0])], sems.at[pl.ds(5, 1)])
    back_terms(local_ref, hub_ref, lr_ref, panel_ref, term_ref, acc_ref, back_ref)
    contributions(cores, blocks_ref, back_ref, panel_ref, keep_ref, send_ref)
    done += fetch(
        [(send_ref, outs[3]), (keep_ref, outs[2]), (back_ref, outs[1])], sems.at[pl.ds(6, 3)]
    )
    for copy in done:
        copy.wait()


def merge_kernel(cores, tile, per_chip, blocks_ref, in_ref, *rest):
    *_, out_hbm, out_ref, sems = rest
    me, core = lax.axis_index("row"), lax.axis_index("col")
    chips, rows, _ = in_ref.shape
    hub = (core * (chips * rows) + position(me, chips) * rows) // tile
    owner = position(blocks_ref[hub] // per_chip, chips)

    def add(p, total):
        return total + jnp.where(p == owner, 0.0, in_ref[p].astype(F32))

    def put(p, carry):
        out_ref[p] = jnp.where(p == owner, total, state)
        pltpu.make_async_copy(out_ref.at[p], out_hbm.at[p], sems.at[p]).start()
        return carry

    def finish(p, carry):
        pltpu.make_async_copy(out_ref.at[p], out_hbm.at[p], sems.at[p]).wait()
        return carry

    zero = jnp.zeros(in_ref.shape[1:], F32)
    total = lax.fori_loop(0, chips, add, zero, unroll=chips <= 16).astype(BF16)
    state = in_ref[owner]
    lax.fori_loop(0, chips, put, 0, unroll=chips <= 16)
    lax.fori_loop(0, chips, finish, 0, unroll=chips <= 16)


def band_kernel(
    cores,
    blocks_ref,
    local_ref,
    hub_ref,
    current_hbm,
    zscores_hbm,
    ridge_hbm,
    band_hbm,
    mine_hbm,
    other_hbm,
    back_hbm,
    back_other_hbm,
    lr_hbm,
    next_hbm,
    chip_ref,
    current_ref,
    zscores_ref,
    ridge_ref,
    band_ref,
    back_ref,
    back_other_ref,
    lr_ref,
    next_ref,
    sems,
):
    me, core = lax.axis_index("row"), lax.axis_index("col")
    blocks, width, tile, _ = band_ref.shape
    rows = blocks * tile
    reach = width // 2
    hubs = blocks_ref.shape[0]
    mine = pl.ds(pl.multiple_of(core * rows, rows), rows)
    other = pl.ds(pl.multiple_of((1 - core) * rows, rows), rows)
    ahead = [
        (mine_hbm, chip_ref.at[mine]),
        (other_hbm, chip_ref.at[other]),
        (band_hbm, band_ref),
    ]
    behind = [
        (current_hbm, current_ref),
        (zscores_hbm, zscores_ref),
        (ridge_hbm, ridge_ref),
        (lr_hbm, lr_ref),
    ]
    extra, store = len(ahead) + len(behind), len(ahead) + len(behind) + 2 * hubs
    early = fetch(ahead, sems)
    late = fetch(behind, sems.at[pl.ds(len(ahead), len(behind))])

    def owned(hub):
        place = Place(blocks_ref[hub], blocks, cores)
        return (place.chip == me) & (place.core == core), place.blk

    def sums(hub):
        row = pl.ds(hub * tile, tile)
        return [
            pltpu.make_async_copy(back_hbm.at[row], back_ref.at[row], sems.at[extra + 2 * hub]),
            pltpu.make_async_copy(
                back_other_hbm.at[row], back_other_ref.at[row], sems.at[extra + 2 * hub + 1]
            ),
        ]

    for hub in range(hubs):

        @pl.when(owned(hub)[0])
        def _():
            for copy in sums(hub):
                copy.start()

    for copy in early:
        copy.wait()

    def product(b, at):
        low, high = max(0, at - reach), min(cores * blocks, at + reach + 1)
        tiles = [band_ref[b, c - at + reach] for c in range(low, high)]
        return dot(jnp.concatenate(tiles, axis=1), chip_ref[low * tile : high * tile, :])

    for n in range(cores):

        @pl.when(core == n)
        def _():
            for b in range(blocks):
                next_ref[b * tile : (b + 1) * tile, :] = product(b, n * blocks + b)

    for copy in late:
        copy.wait()
    for b in range(blocks):
        out = slice(b * tile, (b + 1) * tile)
        current = current_ref[out, :]
        gradient = next_ref[out, :] + (ridge_ref[...] * current - zscores_ref[out, :])
        next_ref[out, :] = current - STEP * gradient

    for hub in range(hubs):
        here, blk = owned(hub)
        row = pl.ds(hub * tile, tile)
        own = pl.ds(pl.multiple_of(blk * tile, tile), tile)

        @pl.when(here)
        def _():
            for copy in sums(hub):
                copy.wait()
            both = back_ref[row, :].astype(F32) + back_other_ref[row, :].astype(F32)
            next_ref[own, :] -= STEP * both

    for s in range(lr_ref.shape[0]):
        block = blocks_ref[hub_ref[s]]
        row = pl.ds(pl.multiple_of(local_ref[s] * tile, tile), tile)

        @pl.when(Place(block, blocks, cores).chip == me)
        def _():
            at = pl.ds(pl.multiple_of((block - me * (cores * blocks)) * tile, tile), tile)
            next_ref[row, :] -= STEP * dot(lr_ref[s], chip_ref[at, :])

    done = pltpu.make_async_copy(next_ref, next_hbm, sems.at[store])
    done.start()
    done.wait()


def step_kernel(
    cores,
    last,
    blocks_ref,
    local_ref,
    hub_ref,
    lr_ref,
    half_ref,
    half_other_ref,
    partial_hbm,
    outer_hbm,
    band_hbm,
    *rest,
):
    if last:
        next_hbm, rest = rest[0], rest[1:]
    else:
        (next_hbm, panel_hbm, back_hbm, keep_ref, send_ref), rest = rest[:5], rest[5:]
    partial_ref, panel_ref, state_ref, grad_ref, term_ref, next_ref, edge_ref, sems = rest
    me, core = lax.axis_index("row"), lax.axis_index("col")
    count, tile, _ = lr_ref.shape
    rows = next_ref.shape[0]
    blocks = rows // tile
    hubs = blocks_ref.shape[0]
    half = half_ref.shape[0]
    reach = edge_ref.shape[1]
    first_edge = (band_hbm.shape[1] - reach) * core
    copies = fetch(
        [
            (outer_hbm, panel_ref),
            (band_hbm.at[:, pl.ds(first_edge, reach)], edge_ref),
            (partial_hbm, partial_ref),
        ],
        sems,
    )
    near = pl.ds(pl.multiple_of(core * half, half), half)
    away = pl.ds(pl.multiple_of((1 - core) * half, half), half)
    state_ref[near, :] = half_ref[...]
    state_ref[away, :] = half_other_ref[...]

    def edge(b, skip, low, high):
        tiles = [edge_ref[b, skip + n] for n in range(high - low)]
        return dot(jnp.concatenate(tiles, axis=1), panel_ref[low * tile : high * tile, :])

    copies[0].wait()
    copies[1].wait()

    @pl.when(core == 0)
    def _():
        for b in range(blocks):
            grad_ref[b * tile : (b + 1) * tile, :] = edge(b, 0, b, blocks)

    @pl.when(core != 0)
    def _():
        for b in range(blocks):
            grad_ref[b * tile : (b + 1) * tile, :] = edge(b, blocks - 1 - b, 0, b + 1)

    for hub in range(hubs):
        place = Place(blocks_ref[hub], blocks, cores)
        own = pl.ds(pl.multiple_of(place.blk * tile, tile), tile)
        row = pl.ds(hub * tile, tile)

        @pl.when((place.chip == me) & (place.core == core))
        def _():
            grad_ref[own, :] += state_ref[row, :].astype(F32)

        @pl.when(place.chip == me)
        def _():
            state_ref[row, :] = jnp.zeros_like(state_ref[row, :])

    for s in range(count):
        col = pl.ds(pl.multiple_of(hub_ref[s] * tile, tile), tile)
        term_ref[s] = dot(lr_ref[s], state_ref[col, :])
    for s in range(count):
        grad_ref[pl.ds(pl.multiple_of(local_ref[s] * tile, tile), tile), :] += term_ref[s]

    copies[2].wait()
    done = []
    for b in range(blocks):
        out = pl.ds(b * tile, tile)
        following = partial_ref[out, :] - STEP * grad_ref[out, :]
        next_ref[out, :] = following
        done += fetch([(next_ref.at[out], next_hbm.at[out])], sems.at[pl.ds(3 + b, 1)])
        if not last:
            panel_ref[out, :] = following.astype(BF16)
    if not last:
        back_ref, acc_ref = state_ref, grad_ref
        done += fetch([(panel_ref, panel_hbm)], sems.at[pl.ds(3 + blocks, 1)])
        back_terms(local_ref, hub_ref, lr_ref, panel_ref, term_ref, acc_ref, back_ref)
        done += fetch([(back_ref, back_hbm)], sems.at[pl.ds(4 + blocks, 1)])
        contributions(cores, blocks_ref, back_ref, panel_ref, keep_ref, send_ref)
    for copy in done:
        copy.wait()


def join_kernel(keep_ref, came_ref, out_ref):
    out_ref[...] = (keep_ref[...].astype(F32) + came_ref[...].astype(F32)).astype(BF16)


def shards(rows_dev, cores, effects, zscores, ridge, band, lr, lr_local, lr_hub, hub_blocks):
    blocks, _, tile, _ = band.shape
    rows, traits = effects.shape
    hubs = hub_blocks.shape[0]
    hub_rows = hubs * tile
    half = hub_rows // cores
    total = rows_dev * cores
    panel_type = jax.ShapeDtypeStruct((rows, traits), BF16)
    back_type = jax.ShapeDtypeStruct((hub_rows, traits), BF16)
    ridge = ridge[None, :]

    odd = [(i, i + 1) for i in range(cores - 1, total - 1, cores)]
    odd = odd + [(j, i) for i, j in odd]
    swap = [(0, 1), (1, 0)]

    def other_core(x):
        return lax.ppermute(x, "col", swap)

    def exchange(x):
        x = x.reshape(rows_dev, half // rows_dev, traits)
        order = ORDERS.get(rows_dev)
        return lax.all_to_all(x, "row", 0, 0, axis_index_groups=order and [list(order)])

    half_type = jax.ShapeDtypeStruct((half, traits), BF16)
    panels, back, keep, send = pl.pallas_call(
        functools.partial(first_kernel, cores),
        out_shape=(panel_type, back_type, half_type, half_type),
        in_specs=[HBM] * 5,
        out_specs=(HBM,) * 4,
        scratch_shapes=[
            pltpu.VMEM((hub_rows, traits), F32),
            pltpu.SMEM(hub_blocks.shape, jnp.int32),
            pltpu.SMEM(lr_local.shape, jnp.int32),
            pltpu.SMEM(lr_hub.shape, jnp.int32),
            pltpu.VMEM(effects.shape, F32),
            pltpu.VMEM(lr.shape, BF16),
            pltpu.SemaphoreType.DMA((9,)),
            pltpu.VMEM((lr.shape[0], tile, traits), F32),
            pltpu.VMEM((rows, traits), BF16),
            pltpu.VMEM((hub_rows, traits), BF16),
            pltpu.VMEM((half, traits), BF16),
            pltpu.VMEM((half, traits), BF16),
        ],
        compiler_params=FIRST,
        name="first",
    )(hub_blocks, lr_local, lr_hub, effects, lr)

    current = effects
    for sweep in range(ITERS):
        last = sweep == ITERS - 1
        outer = lax.ppermute(panels, ("row", "col"), odd)
        came = other_core(send)
        other = other_core(panels)
        back_other = other_core(back)
        chosen = pl.pallas_call(
            join_kernel,
            out_shape=half_type,
            in_specs=[VMEM] * 2,
            out_specs=VMEM,
            compiler_params=MERGE,
            name="join",
        )(keep, came)
        gathered = exchange(chosen)
        merged = pl.pallas_call(
            functools.partial(merge_kernel, cores, tile, blocks * cores),
            out_shape=jax.ShapeDtypeStruct(gathered.shape, BF16),
            in_specs=[SMEM, VMEM, ANY, ANY],
            out_specs=HBM,
            scratch_shapes=[
                pltpu.VMEM(gathered.shape, BF16),
                pltpu.SemaphoreType.DMA((rows_dev,)),
            ],
            compiler_params=MERGE,
            name="merge",
        )(hub_blocks, gathered, other, back_other)
        partial = pl.pallas_call(
            functools.partial(band_kernel, cores),
            out_shape=jax.ShapeDtypeStruct((rows, traits), F32),
            in_specs=[SMEM] * 3 + [HBM] * 9,
            out_specs=HBM,
            scratch_shapes=[
                pltpu.VMEM((cores * rows, traits), BF16),
                pltpu.VMEM(current.shape, F32),
                pltpu.VMEM(zscores.shape, F32),
                pltpu.VMEM(ridge.shape, F32),
                pltpu.VMEM(band.shape, BF16),
                pltpu.VMEM(back.shape, BF16),
                pltpu.VMEM(back.shape, BF16),
                pltpu.VMEM(lr.shape, BF16),
                pltpu.VMEM((rows, traits), F32),
                pltpu.SemaphoreType.DMA((8 + 2 * hubs,)),
            ],
            compiler_params=BAND,
            cost_estimate=pl.CostEstimate(
                flops=10**6, bytes_accessed=2**20, transcendentals=0
            ),
            name="band",
        )(
            hub_blocks,
            lr_local,
            lr_hub,
            current,
            zscores,
            ridge,
            band,
            panels,
            other,
            back,
            back_other,
            lr,
        )
        mine = exchange(merged).reshape(half, traits)
        mine, partial, outer = lax.optimization_barrier((mine, partial, outer))
        theirs = other_core(mine)
        out_shape, out_specs = [jax.ShapeDtypeStruct((rows, traits), F32)], [HBM]
        if not last:
            out_shape += [panel_type, back_type, half_type, half_type]
            out_specs += [HBM, HBM, VMEM, VMEM]
        result = pl.pallas_call(
            functools.partial(step_kernel, cores, last),
            out_shape=tuple(out_shape),
            in_specs=[SMEM] * 3 + [VMEM] * 3 + [HBM] * 3,
            out_specs=tuple(out_specs),
            scratch_shapes=[
                pltpu.VMEM((rows, traits), F32),
                pltpu.VMEM((rows, traits), BF16),
                pltpu.VMEM((hub_rows, traits), BF16),
                pltpu.VMEM((max(rows, hub_rows), traits), F32),
                pltpu.VMEM((lr.shape[0], tile, traits), F32),
                pltpu.VMEM((rows, traits), F32),
                pltpu.VMEM((blocks, band.shape[1] // 2, tile, tile), BF16),
                pltpu.SemaphoreType.DMA((blocks + 5,)),
            ],
            compiler_params=UPDATE,
            name="step",
        )(
            hub_blocks,
            lr_local,
            lr_hub,
            lr,
            mine,
            theirs,
            partial,
            outer,
            band,
        )
        if last:
            return result[0]
        current, panels, back, keep, send = result


def solution(mesh):
    every = ("groups", "row", "col")
    placed = (
        P(every, None),
        P(every, None),
        P("groups"),
        P(every, None, None, None),
        P(every, None, None),
        P(every),
        P(every),
        P("groups"),
    )
    return jax.shard_map(
        functools.partial(shards, mesh.shape["row"], mesh.shape["col"]),
        mesh=mesh,
        in_specs=placed,
        out_specs=P(every, None),
        check_vma=False,
    )
```
